128 devices in a mesh: gx: 16 (over x, y), gy: 8 (over z, core).
Axes of the slice: x: 4, y: 4, z: 4, core: 2. Of those that a mesh axis runs over, the one named last changes fastest.
Arguments:
- thermal_deviation: float32 [2048, 512, 128], P('gx', 'gy'), may hold values from -6 to 6
- darcy_flux: bfloat16 [3, 2048, 512, 128], P(None, 'gx', 'gy'), may hold values from -1 to 1
- mixing_coefficient: bfloat16 [2, 2048, 512, 128], P(None, 'gx', 'gy'), may hold values from 0.049804688 to 0.59765625
- well_patch_site: int32 [16, 8, 128, 8], P('gx', 'gy'), may hold values from 0 to 8191, as said below
- well_stratum_first: int32 [16, 8, 128, 8], P('gx', 'gy'), may hold values from 0 to 31, as said below
- well_stratum_stop: int32 [16, 8, 128, 8], P('gx', 'gy'), may hold values from 0 to 95, as said below
- arriving_entry_lookup: int32 [16, 8, 1024], P('gx', 'gy'), may hold values from 0 to 1024, as said below
- arrived_circuit_order: int32 [16, 8, 1024], P('gx', 'gy'), may hold values from 0 to 1024, as said below
- circuit_solver_operator: float32 [16, 8, 32, 32, 32], P('gx', 'gy')
Outputs:
- new_temperature: float32 [2048, 512, 128], P('gx', 'gy')
- heat_rates: float32 [16, 8, 1024, 128], P('gx', 'gy')
The draws below stay inside these ranges and needn't reach their ends.
Inputs may be any that keep to these rules, and one draw needn't show every extreme that they name: `well_patch_site`: A cell within one tile. A slot is live when well_stratum_stop > well_stratum_first; dead slots have both 0. For each tile and owner the live slots are slots 0 to n - 1 with n from 1 to 8; n is 8 for a tile's own owner index. Live boreholes span 128 // 4 to 64 layers starting above layer 32. `well_stratum_stop`: see well_stratum_first. `arriving_entry_lookup`: each live received slot fills exactly one loop position; unfilled positions hold 1024. `arrived_circuit_order`: the inverse of arriving_entry_lookup on live slots; dead received slots hold 1024.
All inputs are finite; a program needn't handle non-finite values.
Results may differ from the reference program's by a relative error of at most 0.0003.
Values sent between devices are 32-bit elements; how exact they have to be, the bound alone decides.
A program may use at most 192 MiB of HBM per device.

```python
import math
import jax
import jax.numpy as jnp
from jax import lax

CX = 128
CY = 64
STRATA_COUNT = 128
CAP = 8
BLD_DEV = 32
BMAX = 32
STEPS = 2
MESH_COUNT_EAST = 2048
MESH_COUNT_NORTH = 512
N_GX = 16
N_GY = 8


def layout_tables(key):
    groups = N_GX * N_GY
    counts = jax.random.randint(jax.random.fold_in(key, 1), (groups, groups), 1, CAP + 1)
    index = jnp.arange(groups, dtype=jnp.int32)
    counts = jnp.where((index[:, None] + 1) % groups == index[None, :], 1, counts)
    counts = jnp.where(index[:, None] == index[None, :], CAP, counts)
    live = jnp.arange(CAP, dtype=jnp.int32)[None, None, :] < counts[:, :, None]
    start = jax.random.randint(jax.random.fold_in(key, 2), (groups, groups, CAP), 0, STRATA_COUNT // 4)
    length = jax.random.randint(jax.random.fold_in(key, 3), (groups, groups, CAP), STRATA_COUNT // 4, STRATA_COUNT // 2 + 1)
    top = jnp.where(live, start, 0).astype(jnp.int32)
    bottom = jnp.where(live, start + length, 0).astype(jnp.int32)
    owner_live = live.transpose(1, 0, 2).reshape(groups, groups * CAP)
    order = jnp.cumsum(owner_live.astype(jnp.int32), axis=1) - 1
    base = jax.random.fold_in(key, 4)

    def one_owner(owner, alive, rank):
        perm = jax.random.permutation(jax.random.fold_in(base, owner), BLD_DEV * BMAX).astype(jnp.int32)
        place = jnp.where(alive, perm[jnp.clip(rank, 0, BLD_DEV * BMAX - 1)], BLD_DEV * BMAX).astype(jnp.int32)
        filled = jnp.full((BLD_DEV * BMAX,), groups * CAP, jnp.int32)
        filled = filled.at[place].set(jnp.arange(groups * CAP, dtype=jnp.int32), mode='drop')
        return (filled, place)
    gathered, placed = jax.vmap(one_owner)(index, owner_live, order)
    return (top, bottom, gathered, placed)


def draw_well_patch_site(key, part):
    groups = N_GX * N_GY
    return jax.random.randint(jax.random.fold_in(key, 7), (N_GX, N_GY, groups, CAP), 0, CX * CY).astype(jnp.int32)


def draw_well_stratum_first(key, part):
    top, bottom, gathered, placed = layout_tables(key)
    return top.reshape(N_GX, N_GY, N_GX * N_GY, CAP)


def draw_well_stratum_stop(key, part):
    top, bottom, gathered, placed = layout_tables(key)
    return bottom.reshape(N_GX, N_GY, N_GX * N_GY, CAP)


def draw_arriving_entry_lookup(key, part):
    top, bottom, gathered, placed = layout_tables(key)
    return gathered.reshape(N_GX, N_GY, BLD_DEV * BMAX)


def draw_arrived_circuit_order(key, part):
    top, bottom, gathered, placed = layout_tables(key)
    return placed.reshape(N_GX, N_GY, N_GX * N_GY * CAP)


def draw_circuit_solver_operator(key, part):
    array_shape = (N_GX, N_GY, BLD_DEV, BMAX, BMAX)
    diagonal = jax.random.uniform(jax.random.fold_in(key, 11), array_shape, jnp.float32, 0.3, 0.6)
    spread = 0.12 * jax.random.normal(jax.random.fold_in(key, 12), array_shape, jnp.float32)
    identity = jnp.eye(BMAX, dtype=jnp.float32)
    return (spread * (1.0 - identity) + diagonal * identity).astype(jnp.float32)


def level_of(stream_key, extent, cuts, smallest, largest):
    factor_of = 1.0
    for position, parts in cuts:
        draws = jax.random.uniform(jax.random.fold_in(jax.random.fold_in(stream_key, 6), position), (parts,), jnp.float32, smallest / len(cuts), largest / len(cuts))
        factor_of = factor_of * jnp.repeat(jnp.exp(draws), extent[position] // parts).reshape((-1,) + (1,) * (len(extent) - 1 - position))
    return factor_of


def scatter_about(own_key, extent, scale, most, pieces=(), held_as=jnp.bfloat16):
    array = jax.random.normal(own_key, extent, jnp.float32) * scale
    if len(pieces) > 0:
        array = level_of(own_key, extent, pieces, -0.22, 0.18) * array
    return jnp.clip(array, min=-most, max=most).astype(held_as)


def setup_inputs(seed: int = 0) -> dict:
    key_of = jax.random.split(jax.random.key(seed), 10)
    return {
        "thermal_deviation": scatter_about(key_of[0], (MESH_COUNT_EAST, MESH_COUNT_NORTH, STRATA_COUNT), 1.0, 6.0, ((0, 16), (1, 8)), jnp.float32),
        "darcy_flux": jnp.clip(jax.random.uniform(key_of[1], (3, MESH_COUNT_EAST, MESH_COUNT_NORTH, STRATA_COUNT), jnp.float32, -1.0, 1.0) * level_of(key_of[1], (3, MESH_COUNT_EAST, MESH_COUNT_NORTH, STRATA_COUNT), ((1, 16), (2, 8)), -0.4, 0.0), -1.0, 1.0).astype(jnp.bfloat16),
        "mixing_coefficient": jnp.clip(jnp.exp(math.log(0.59765625) - 2.4849066 * jax.random.uniform(key_of[2], (2, MESH_COUNT_EAST, MESH_COUNT_NORTH, STRATA_COUNT), jnp.float32) ** level_of(key_of[2], (2, MESH_COUNT_EAST, MESH_COUNT_NORTH, STRATA_COUNT), ((1, 16), (2, 8)), -0.2, 0.2)), 0.049804688, 0.59765625).astype(jnp.bfloat16),
        "well_patch_site": draw_well_patch_site(jax.random.fold_in(key_of[9], 71), 0),
        "well_stratum_first": draw_well_stratum_first(jax.random.fold_in(key_of[9], 71), 0),
        "well_stratum_stop": draw_well_stratum_stop(jax.random.fold_in(key_of[9], 71), 0),
        "arriving_entry_lookup": draw_arriving_entry_lookup(jax.random.fold_in(key_of[9], 71), 0),
        "arrived_circuit_order": draw_arrived_circuit_order(jax.random.fold_in(key_of[9], 71), 0),
        "circuit_solver_operator": draw_circuit_solver_operator(jax.random.fold_in(key_of[9], 71), 0),
    }


def tendency(padded, darcy_flux, mixing_coefficient):
    full = jnp.pad(padded, ((0, 0), (0, 0), (1, 1)))
    centre = full[1:-1, 1:-1, 1:-1]
    x_minus = full[:-2, 1:-1, 1:-1]
    x_plus = full[2:, 1:-1, 1:-1]
    y_minus = full[1:-1, :-2, 1:-1]
    y_plus = full[1:-1, 2:, 1:-1]
    z_minus = full[1:-1, 1:-1, :-2]
    z_plus = full[1:-1, 1:-1, 2:]
    speed = darcy_flux.astype(jnp.float32)
    coeff = mixing_coefficient.astype(jnp.float32)
    advect = jnp.maximum(speed[0], 0.0) * (centre - x_minus) + jnp.minimum(speed[0], 0.0) * (x_plus - centre)
    advect = advect + jnp.maximum(speed[1], 0.0) * (centre - y_minus) + jnp.minimum(speed[1], 0.0) * (y_plus - centre)
    advect = advect + jnp.maximum(speed[2], 0.0) * (centre - z_minus) + jnp.minimum(speed[2], 0.0) * (z_plus - centre)
    spread = coeff[0] * (x_plus + x_minus + y_plus + y_minus - 4.0 * centre) + coeff[1] * (z_plus + z_minus - 2.0 * centre)
    return 0.1 * (spread - advect)


def reference(thermal_deviation, darcy_flux, mixing_coefficient, well_patch_site, well_stratum_first, well_stratum_stop, arriving_entry_lookup, arrived_circuit_order, circuit_solver_operator):
    groups = N_GX * N_GY
    tile_x = jnp.arange(N_GX, dtype=jnp.int32)[:, None, None, None]
    tile_y = jnp.arange(N_GY, dtype=jnp.int32)[None, :, None, None]
    cell_x = tile_x * CX + well_patch_site // CY
    cell_y = tile_y * CY + well_patch_site % CY
    layers = jnp.arange(STRATA_COUNT, dtype=jnp.int32)
    masks = ((layers >= well_stratum_first[..., None]) & (layers < well_stratum_stop[..., None])).astype(jnp.float32)
    gather_flat = arriving_entry_lookup.reshape(groups, BLD_DEV * BMAX)
    return_flat = arrived_circuit_order.reshape(groups, groups * CAP)
    inverse = circuit_solver_operator.reshape(groups, BLD_DEV, BMAX, BMAX)
    pick = jax.vmap(lambda rows, index: rows[index])
    thermal_state = thermal_deviation
    rates = None
    for step in range(STEPS):
        padded = jnp.pad(thermal_state, ((1, 1), (1, 1), (0, 0)))
        rate = tendency(padded, darcy_flux, mixing_coefficient)
        columns = thermal_state[cell_x, cell_y] * masks
        received = columns.reshape(groups, groups, CAP, STRATA_COUNT).transpose(1, 0, 2, 3).reshape(groups, groups * CAP, STRATA_COUNT)
        received = jnp.concatenate([received, jnp.zeros((groups, 1, STRATA_COUNT), jnp.float32)], axis=1)
        loops = pick(received, gather_flat).reshape(groups, BLD_DEV, BMAX, STRATA_COUNT)
        rates = jnp.einsum("dbjk,dbkz->dbjz", inverse, loops, precision=lax.Precision.HIGHEST)
        rates = rates.reshape(groups, BLD_DEV * BMAX, STRATA_COUNT)
        extended = jnp.concatenate([rates, jnp.zeros((groups, 1, STRATA_COUNT), jnp.float32)], axis=1)
        back = pick(extended, return_flat).reshape(groups, groups, CAP, STRATA_COUNT).transpose(1, 0, 2, 3)
        back = back.reshape(N_GX, N_GY, groups, CAP, STRATA_COUNT) * masks
        deposit = jnp.zeros((MESH_COUNT_EAST, MESH_COUNT_NORTH, STRATA_COUNT), jnp.float32).at[cell_x, cell_y].add(back)
        thermal_state = thermal_state + rate - deposit
    return thermal_state, rates.reshape(N_GX, N_GY, BLD_DEV * BMAX, STRATA_COUNT)
```

```python
import functools

import jax
import jax.numpy as jnp
from jax import lax
from jax.experimental import pallas as pl
from jax.experimental.pallas import tpu as pltpu
from jax.sharding import PartitionSpec as P

MESH = pl.DeviceIdType.MESH
F32 = jnp.float32
BF16 = jnp.bfloat16

NX, NY, NZ = 128, 64, 128
CELLS = NX * NY
GROUPS, CAP = 128, 8
SLOTS = GROUPS * CAP
HALF = 64

HOPS = (0, 1, 2, 1)
OFFSETS = sorted(
    [(a, b, c, d) for a in range(4) for b in range(4) for c in range(4) for d in range(2)][1:],
    key=lambda o: -(HOPS[o[0]] + HOPS[o[1]] + HOPS[o[2]] + 0.3 * o[3]),
)


def iota(shape, dim):
    return lax.broadcasted_iota(jnp.int32, shape, dim)


def dot(a, b):
    return jnp.dot(a, b, preferred_element_type=F32)


def parts_of(x):
    hi = x.astype(BF16)
    return hi, (x - hi.astype(F32)).astype(BF16)


def one_hot(mask):
    return jnp.where(mask, 1.0, 0.0).astype(BF16)


def spread(table, first_lane):
    slot, lane = iota((SLOTS, 128), 0), iota((SLOTS, 128), 1)
    rows = dot(one_hot(slot // CAP == lane), table.astype(BF16))
    own = jnp.where(lane == first_lane + slot % CAP, rows, 0.0).astype(BF16)
    return dot(own, jnp.ones((128, 128), BF16)).astype(jnp.int32)


def rate_of(c, xm, xp, ym, yp, flux, mix):
    vx, vy, vz = flux
    kh, kv = mix
    lane = iota((NY, NZ), 1)
    zm = jnp.where(lane == 0, 0.0, pltpu.roll(c, 1, 1))
    zp = jnp.where(lane == NZ - 1, 0.0, pltpu.roll(c, NZ - 1, 1))
    total = (kh - jnp.minimum(vx, 0.0)) * (xp - c) - (kh + jnp.maximum(vx, 0.0)) * (c - xm)
    total += (kh - jnp.minimum(vy, 0.0)) * (yp - c) - (kh + jnp.maximum(vy, 0.0)) * (c - ym)
    total += (kv - jnp.minimum(vz, 0.0)) * (zp - c) - (kv + jnp.maximum(vz, 0.0)) * (c - zm)
    return c + 0.1 * total


def transport(
    site,
    u_hbm,
    flux_hbm,
    mix_hbm,
    first_ref,
    stop_ref,
    site_row,
    lookup_row,
    order_row,
    solver_ref,
    grid_out,
    columns_out,
    heat_out,
    state,
    after,
    flux,
    mix,
    xhalo,
    yhalo,
    yface,
    columns,
    base,
    masks,
    pack_own,
    unpack_own,
    pack_got,
    unpack_got,
    table,
    lookup_mat,
    return_mat,
    cell_mat,
    blocks,
    rhs,
    out_box,
    in_box,
    out_one,
    in_one,
    load_sem,
    store_sem,
    halo_send,
    halo_recv,
    send_sem,
    recv_sem,
):
    gx, gy = lax.axis_index("gx"), lax.axis_index("gy")
    me = gx * 8 + gy
    px, py = lax.div(gx, 4), lax.rem(gx, 4)
    pz, pc = lax.div(gy, 2), lax.rem(gy, 2)
    xs = [lax.rem(px + i, 4) for i in range(4)]
    ys = [lax.rem(py + i, 4) for i in range(4)]
    zs = [lax.rem(pz + i, 4) for i in range(4)]
    cs = [lax.rem(pc + i, 2) for i in range(2)]
    peers = [(xs[a] * 4 + ys[b], zs[c] * 2 + cs[d]) for a, b, c, d in OFFSETS]

    load_u = pltpu.make_async_copy(u_hbm, state, load_sem.at[0])
    load_flux = pltpu.make_async_copy(flux_hbm, flux, load_sem.at[1])
    load_mix = pltpu.make_async_copy(mix_hbm, mix, load_sem.at[2])
    load_u.start()
    load_flux.start()
    load_mix.start()
    barrier = pltpu.get_barrier_semaphore()
    for peer in peers:
        pl.semaphore_signal(barrier, inc=1, device_id=peer, device_id_type=MESH)

    lane8 = iota((CAP, 128), 1)

    def pack(index, box, width):
        def group(o, carry):
            rows = pl.ds(pl.multiple_of(o * CAP, CAP), CAP)
            cut = jnp.take_along_axis(columns[rows, :], index[rows, :], axis=1)
            box[o, 0:4, :] = jnp.where(lane8[0:4] < HALF, cut[0:4], cut[4:8])
            return carry

        lax.fori_loop(0, GROUPS, group, 0, unroll=8)

    def unpack(box, index, keep):
        def group(o, carry):
            rows = pl.ds(pl.multiple_of(o * CAP, CAP), CAP)
            half = box[o, 0:4, :]
            both = jnp.concatenate([half, half], axis=0)
            wide = jnp.take_along_axis(both, index[rows, :], axis=1)
            wide = wide * keep(rows)
            columns[rows, :] = wide
            return carry

        lax.fori_loop(0, GROUPS, group, 0, unroll=8)

    def indices(first, pack_ref, unpack_ref):
        lane = iota((SLOTS, 128), 1)
        shift = jnp.where(iota((SLOTS, 128), 0) % CAP >= 4, HALF, 0)
        pack_ref[...] = (lane + first + shift) & 127
        unpack_ref[...] = (lane - first + shift) & 127

    def send(box, landing, k):
        for x, y in peers:
            pltpu.make_async_remote_copy(
                box.at[x * 8 + y],
                landing.at[me],
                send_sem.at[k],
                recv_sem.at[k],
                device_id=(x, y),
                device_id_type=MESH,
            ).start()
        landing[me] = box[me]

    def receive(box, landing, k):
        some = landing.at[pl.ds(0, GROUPS - 1)]
        pltpu.make_async_copy(some, some, recv_sem.at[k]).wait()

    def sent(box, k):
        some = box.at[pl.ds(0, GROUPS - 1)]
        pltpu.make_async_copy(some, some, send_sem.at[k]).wait()

    def halo_copies(step):
        low_x, high_x = state.at[pl.ds(0, NY)], state.at[pl.ds(CELLS - NY, NY)]
        low_y, high_y = yface.at[step, 0], yface.at[step, 1]
        plan = [
            (gx > 0, low_x, xhalo.at[step, 1], 1, (gx - 1, gy)),
            (gx < 15, high_x, xhalo.at[step, 0], 0, (gx + 1, gy)),
            (gy > 0, low_y, yhalo.at[step, 1], 3, (gx, gy - 1)),
            (gy < 7, high_y, yhalo.at[step, 0], 2, (gx, gy + 1)),
        ]
        return [
            (
                there,
                pltpu.make_async_remote_copy(
                    source,
                    target,
                    halo_send.at[step, side],
                    halo_recv.at[step, side],
                    device_id=device,
                    device_id_type=MESH,
                ),
            )
            for there, source, target, side, device in plan
        ]

    def halo_start(step):
        def face(i, carry):
            yface[step, 0, pl.ds(i, 1), :] = state[pl.ds(i * NY, 1), :]
            yface[step, 1, pl.ds(i, 1), :] = state[pl.ds(i * NY + NY - 1, 1), :]
            return carry

        lax.fori_loop(0, NX, face, 0, unroll=8)
        for there, copy in halo_copies(step):

            @pl.when(there)
            def _():
                copy.start()

    def halo_wait(step):
        for there, copy in halo_copies(step):

            @pl.when(there)
            def _():
                copy.wait_send()

        for there, side in ((gx > 0, 0), (gx < 15, 1), (gy > 0, 2), (gy < 7, 3)):
            block = xhalo.at[step, side] if side < 2 else yhalo.at[step, side - 2]

            @pl.when(there)
            def _():
                pltpu.make_async_copy(block, block, halo_recv.at[step, side]).wait()

    def stencil(step):
        row = iota((NY, NZ), 0)

        def slab(i, xm, xp):
            here = pl.ds(pl.multiple_of(i * NY, NY), NY)
            c = state[here, :]
            ym = jnp.where(row == 0, yhalo[step, 0, pl.ds(i, 1), :], pltpu.roll(c, 1, 0))
            yp = jnp.where(row == NY - 1, yhalo[step, 1, pl.ds(i, 1), :], pltpu.roll(c, NY - 1, 0))
            after[here, :] = rate_of(
                c,
                xm,
                xp,
                ym,
                yp,
                [flux[d, here, :].astype(F32) for d in range(3)],
                [mix[d, here, :].astype(F32) for d in range(2)],
            )

        def at(i):
            return state[pl.ds(pl.multiple_of(i * NY, NY), NY), :]

        def inner(i, carry):
            slab(i, at(i - 1), at(i + 1))
            return carry

        slab(0, xhalo[step, 0], at(1))
        lax.fori_loop(1, NX - 1, inner, 0)
        slab(NX - 1, at(NX - 2), xhalo[step, 1])

    def gather(source, target):
        def group(o, carry):
            for c in range(CAP):
                s = o * CAP + c
                target[pl.ds(s, 1), :] = source[pl.ds(site[s], 1), :]
            return carry

        lax.fori_loop(0, GROUPS, group, 0, unroll=4)

    def solve(last):
        hi, lo = parts_of(columns[...])
        rhs[:, 0:128] = hi
        rhs[:, 128:256] = lo
        loops = dot(lookup_mat[...], rhs[...]).astype(BF16)
        for g in range(4):
            rows = slice(g * 256, g * 256 + 256)
            two = dot(blocks[0, rows, :], loops[rows])
            small = dot(blocks[1, rows, :], loops[rows, 0:128])
            rates = two[:, 0:128] + two[:, 128:256] + small
            if last:
                heat_out[rows, :] = rates
            hi, lo = parts_of(rates)
            rhs[rows, 0:128] = hi
            rhs[rows, 128:256] = lo
        two = dot(return_mat[...], rhs[...])
        columns[...] = two[:, 0:128] + two[:, 128:256]

    def deposits():
        hi, lo = parts_of(columns[...])
        rhs[:, 0:128] = hi
        rhs[:, 128:256] = lo
        two = dot(cell_mat[...], rhs[...])
        return two[:, 0:128] + two[:, 128:256]

    table[...] = jnp.zeros_like(table)
    table[:, 0:8] = first_ref[...].astype(F32)
    table[:, 8:16] = stop_ref[...].astype(F32)
    first = spread(table[...], 0)
    stop = spread(table[...], 8)
    layer = iota((SLOTS, 128), 1)
    masks[...] = jnp.where((layer >= first) & (layer < stop), 1.0, 0.0)
    indices(first, pack_own, unpack_own)
    for edge, halo, side in ((gx == 0, xhalo, 0), (gx == 15, xhalo, 1), (gy == 0, yhalo, 0), (gy == 7, yhalo, 1)):

        @pl.when(edge)
        def _():
            halo[:, side] = jnp.zeros_like(halo[:, side])

    load_u.wait()
    gather(state, columns)
    columns[...] = columns[...] * masks[...]
    pack(pack_own, out_one, 5)
    out_one[:, 4, :] = table[...]
    pl.semaphore_wait(barrier, GROUPS - 1)
    halo_start(0)
    send(out_one, in_one, 0)

    def build(o, carry):
        rows = pl.ds(pl.multiple_of(o * 128, 128), 128)
        slot = iota((128, SLOTS), 0) + o * 128
        lookup_mat[rows, :] = one_hot(order_row[...] == slot)
        return_mat[rows, :] = one_hot(lookup_row[...] == slot)
        return carry

    lax.fori_loop(0, 8, build, 0)
    tile = one_hot(iota((32, 256), 1) % 32 == iota((32, 256), 0))
    own_block = (iota((SLOTS, 256), 0) // 32) % 8 == iota((SLOTS, 256), 1) // 32
    for part, piece in enumerate(parts_of(solver_ref[...])):
        blocks[part] = jnp.where(own_block, dot(piece, tile), 0.0).astype(BF16)
    ones = jnp.ones((128, 128), BF16)

    load_flux.wait()
    load_mix.wait()
    halo_wait(0)
    stencil(0)
    receive(out_one, in_one, 0)
    indices(spread(in_one[:, 4, :], 0), pack_got, unpack_got)
    window = lambda index: lambda rows: jnp.where(
        ((index[rows, :] ^ jnp.where(iota((CAP, 128), 0) >= 4, HALF, 0)) & 127) < HALF, 1.0, 0.0
    )
    keep_got = window(unpack_got)
    keep_own = lambda rows: masks[rows, :]
    unpack(in_one, unpack_got, keep_got)
    solve(False)
    pack(pack_got, out_box.at[0], 4)
    send(out_box.at[0], in_box.at[0], 1)

    gather(after, base)

    eye = iota((128, 128), 0) == iota((128, 128), 1)
    for o in range(8):
        piece = site_row[:, o * 128 : (o + 1) * 128]
        upper = jnp.where(eye, lax.shift_right_logical(piece, 6).astype(F32), 0.0).astype(BF16)
        lower = jnp.where(eye, (piece & 63).astype(F32), 0.0).astype(BF16)
        tall = (dot(upper, ones) * 64.0 + dot(lower, ones)).astype(jnp.int32)
        for q in range(8):
            cell_mat[o * 128 : (o + 1) * 128, q * 128 : (q + 1) * 128] = one_hot(
                tall == site_row[:, q * 128 : (q + 1) * 128]
            )

    receive(out_box.at[0], in_box.at[0], 1)
    unpack(in_box.at[0], unpack_own, keep_own)
    base[...] = base[...] - deposits()
    columns[...] = base[...] * masks[...]
    pack(pack_own, out_box.at[1], 4)
    send(out_box.at[1], in_box.at[1], 2)

    def lay(o, carry):
        rows = pl.ds(pl.multiple_of(o * 1024, 1024), 1024)
        pick = one_hot(iota((1024, SLOTS), 0) + o * 1024 == site_row[...])
        two = dot(pick, rhs[...])
        state[rows, :] = after[rows, :] - (two[:, 0:128] + two[:, 128:256])
        return carry

    lax.fori_loop(0, 8, lay, 0)
    halo_start(1)
    receive(out_box.at[1], in_box.at[1], 2)
    unpack(in_box.at[1], unpack_got, keep_got)
    solve(True)
    pack(pack_got, out_box.at[2], 4)
    send(out_box.at[2], in_box.at[2], 3)

    halo_wait(1)
    stencil(1)
    store = pltpu.make_async_copy(after, grid_out, store_sem)
    store.start()
    gather(after, base)
    receive(out_box.at[2], in_box.at[2], 3)
    unpack(in_box.at[2], unpack_own, keep_own)
    columns_out[...] = base[...] - deposits()
    sent(out_one, 0)
    for k in range(3):
        sent(out_box.at[k], k + 1)
    store.wait()


def settle(site, grid_hbm, rows_ref, heat_hbm, out_hbm, heat_out, held, sem):
    heat = pltpu.make_async_copy(heat_hbm, heat_out, sem.at[2])
    heat.start()
    load = pltpu.make_async_copy(grid_hbm, held, sem.at[0])
    load.start()
    load.wait()

    def group(o, carry):
        for c in range(CAP):
            s = o * CAP + c
            held[pl.ds(site[s], 1), :] = rows_ref[pl.ds(s, 1), :]
        return carry

    lax.fori_loop(0, GROUPS, group, 0, unroll=4)
    store = pltpu.make_async_copy(held, out_hbm, sem.at[1])
    store.start()
    store.wait()
    heat.wait()


VMEM = pl.BlockSpec(memory_space=pltpu.VMEM)
SMEM = pl.BlockSpec(memory_space=pltpu.SMEM)
ANY = pl.BlockSpec(memory_space=pl.ANY)


def local(u, flux, mix, site, first, stop, lookup, order, solver):
    u2 = u.reshape(CELLS, NZ)
    flux2 = flux.reshape(3, CELLS, NZ)
    mix2 = mix.reshape(2, CELLS, NZ)
    site1 = site.reshape(SLOTS)
    grid_shape = jax.ShapeDtypeStruct((CELLS, NZ), F32)
    slot_shape = jax.ShapeDtypeStruct((SLOTS, NZ), F32)
    slot_f32 = pltpu.VMEM((SLOTS, NZ), F32)
    slot_i32 = pltpu.VMEM((SLOTS, NZ), jnp.int32)
    square = pltpu.VMEM((SLOTS, SLOTS), BF16)
    grid, rows, heat = pl.pallas_call(
        transport,
        out_shape=(grid_shape, slot_shape, slot_shape),
        in_specs=[SMEM, ANY, ANY, ANY] + [VMEM] * 6,
        out_specs=(ANY, VMEM, VMEM),
        scratch_shapes=[
            pltpu.VMEM((CELLS, NZ), F32),
            pltpu.VMEM((CELLS, NZ), F32),
            pltpu.VMEM((3, CELLS, NZ), BF16),
            pltpu.VMEM((2, CELLS, NZ), BF16),
            pltpu.VMEM((2, 2, NY, NZ), F32),
            pltpu.VMEM((2, 2, NX, NZ), F32),
            pltpu.VMEM((2, 2, NX, NZ), F32),
            slot_f32,
            slot_f32,
            slot_f32,
            slot_i32,
            slot_i32,
            slot_i32,
            slot_i32,
            pltpu.VMEM((GROUPS, 128), F32),
            square,
            square,
            square,
            pltpu.VMEM((2, SLOTS, 256), BF16),
            pltpu.VMEM((SLOTS, 256), BF16),
            pltpu.VMEM((3, GROUPS, 4, NZ), F32),
            pltpu.VMEM((3, GROUPS, 4, NZ), F32),
            pltpu.VMEM((GROUPS, 5, NZ), F32),
            pltpu.VMEM((GROUPS, 5, NZ), F32),
            pltpu.SemaphoreType.DMA((3,)),
            pltpu.SemaphoreType.DMA,
            pltpu.SemaphoreType.DMA((2, 4)),
            pltpu.SemaphoreType.DMA((2, 4)),
            pltpu.SemaphoreType.DMA((4,)),
            pltpu.SemaphoreType.DMA((4,)),
        ],
        compiler_params=pltpu.CompilerParams(
            collective_id=0, has_side_effects=True, vmem_limit_bytes=56 << 20
        ),
    )(
        site1,
        u2,
        flux2,
        mix2,
        first.reshape(GROUPS, CAP),
        stop.reshape(GROUPS, CAP),
        site1.reshape(1, SLOTS),
        lookup.reshape(1, SLOTS),
        order.reshape(1, SLOTS),
        solver.reshape(SLOTS, 32),
    )
    grid, heat = pl.pallas_call(
        settle,
        out_shape=(grid_shape, slot_shape),
        in_specs=[SMEM, ANY, VMEM, ANY],
        out_specs=(ANY, ANY),
        scratch_shapes=[pltpu.VMEM((CELLS, NZ), F32), pltpu.SemaphoreType.DMA((3,))],
        compiler_params=pltpu.CompilerParams(vmem_limit_bytes=16 << 20),
    )(site1, grid, rows, heat)
    return grid.reshape(NX, NY, NZ), heat.reshape(1, 1, SLOTS, NZ)


def solution(mesh):
    placed = (
        P("gx", "gy", None),
        P(None, "gx", "gy", None),
        P(None, "gx", "gy", None),
        P("gx", "gy", None, None),
        P("gx", "gy", None, None),
        P("gx", "gy", None, None),
        P("gx", "gy", None),
        P("gx", "gy", None),
        P("gx", "gy", None, None, None),
    )
    return jax.shard_map(
        local,
        mesh=mesh,
        in_specs=placed,
        out_specs=(P("gx", "gy", None), P("gx", "gy", None, None)),
        check_vma=False,
    )
```

```python
import functools

import jax
import jax.numpy as jnp
from jax import lax
from jax.experimental import pallas as pl
from jax.experimental.pallas import tpu as pltpu
from jax.sharding import PartitionSpec as P

MESH = pl.DeviceIdType.MESH
F32 = jnp.float32
BF16 = jnp.bfloat16

NX, NY, NZ = 128, 64, 128
CELLS = NX * NY
GROUPS, CAP = 128, 8
SLOTS = GROUPS * CAP
HALF = 64

HOPS = (0, 1, 2, 1)
OFFSETS = sorted(
    [(a, b, c, d) for a in range(4) for b in range(4) for c in range(4) for d in range(2)][1:],
    key=lambda o: -(HOPS[o[0]] + HOPS[o[1]] + HOPS[o[2]] + 0.3 * o[3]),
)


def iota(shape, dim):
    return lax.broadcasted_iota(jnp.int32, shape, dim)


def dot(a, b):
    return jnp.dot(a, b, preferred_element_type=F32)


def parts_of(x):
    hi = x.astype(BF16)
    return hi, (x - hi.astype(F32)).astype(BF16)


def one_hot(mask):
    return jnp.where(mask, 1.0, 0.0).astype(BF16)


def tall(row):
    eye = iota((128, 128), 0) == iota((128, 128), 1)
    spread = jnp.where(eye, row.astype(F32), 0.0).astype(BF16)
    return dot(spread, jnp.ones((128, 128), BF16))


def rate_of(c, xm, xp, ym, yp, flux, mix):
    vx, vy, vz = flux
    kh, kv = mix
    lane = iota(c.shape, 1)
    zm = jnp.where(lane == 0, 0.0, pltpu.roll(c, 1, 1))
    zp = jnp.where(lane == NZ - 1, 0.0, pltpu.roll(c, NZ - 1, 1))
    xa, xb, ya, yb, za, zb = xp - c, c - xm, yp - c, c - ym, zp - c, c - zm
    advect = vx * jnp.where(vx > 0.0, xb, xa)
    advect += vy * jnp.where(vy > 0.0, yb, ya)
    advect += vz * jnp.where(vz > 0.0, zb, za)
    return c + 0.1 * (kh * ((xa - xb) + (ya - yb)) + kv * (za - zb) - advect)


def transport(
    site,
    u_hbm,
    flux_hbm,
    mix_hbm,
    first_ref,
    stop_ref,
    site_ref,
    lookup_row,
    solver_hbm,
    grid_out,
    columns_out,
    heat_out,
    state,
    after,
    flux,
    mix,
    xhalo,
    yhalo,
    yface,
    base,
    masks,
    pack_own,
    unpack_own,
    pack_got,
    unpack_got,
    lookup_mat,
    return_mat,
    cell_mat,
    solver,
    blocks,
    rhs,
    heat,
    row_hot,
    pick_a,
    pick_b,
    out_box,
    in_box,
    out_one,
    in_one,
    load_sem,
    store_sem,
    halo_send,
    halo_recv,
    send_sem,
    recv_sem,
):
    gx, gy = lax.axis_index("gx"), lax.axis_index("gy")
    me = gx * 8 + gy
    px, py = lax.div(gx, 4), lax.rem(gx, 4)
    pz, pc = lax.div(gy, 2), lax.rem(gy, 2)
    xs = [lax.rem(px + i, 4) for i in range(4)]
    ys = [lax.rem(py + i, 4) for i in range(4)]
    zs = [lax.rem(pz + i, 4) for i in range(4)]
    cs = [lax.rem(pc + i, 2) for i in range(2)]
    peers = [(xs[a] * 4 + ys[b], zs[c] * 2 + cs[d]) for a, b, c, d in OFFSETS]

    loads = [
        pltpu.make_async_copy(source, target, load_sem.at[i])
        for i, (source, target) in enumerate(
            ((u_hbm, state), (flux_hbm, flux), (mix_hbm, mix), (solver_hbm, solver))
        )
    ]
    for load in loads:
        load.start()
    barrier = pltpu.get_barrier_semaphore()
    for peer in peers:
        pl.semaphore_signal(barrier, inc=1, device_id=peer, device_id_type=MESH)

    lane = iota((128, 128), 1)

    def block(c):
        return slice(c * 128, c * 128 + 128)

    def indices(c, first, pack_ref, unpack_ref):
        shift = HALF if c >= 4 else 0
        pack_ref[block(c), :] = (lane + first + shift) & 127
        unpack_ref[block(c), :] = (lane - first + shift) & 127

    def pack(value, index, box):
        for r in range(4):
            left, right = (
                jnp.take_along_axis(value(c), index[block(c), :], axis=1) for c in (r, r + 4)
            )
            box[:, r, :] = jnp.where(lane < HALF, left, right)

    def unpack(box, index, keep):
        for r in range(4):
            pair = box[:, r, :]
            for c in (r, r + 4):
                wide = jnp.take_along_axis(pair, index[block(c), :], axis=1)
                hi, lo = parts_of(jnp.where(keep(c), wide, 0.0))
                rhs[block(c), 0:128] = hi
                rhs[block(c), 128:256] = lo

    def own(c):
        return masks[block(c), :] > 0.0

    def got(c):
        return ((unpack_got[block(c), :] - (HALF if c >= 4 else 0)) & 127) < HALF

    def send(box, landing, k):
        for x, y in peers:
            pltpu.make_async_remote_copy(
                box.at[x * 8 + y],
                landing.at[me],
                send_sem.at[k],
                recv_sem.at[k],
                device_id=(x, y),
                device_id_type=MESH,
            ).start()
        landing[me] = box[me]

    def receive(landing, k):
        some = landing.at[pl.ds(0, GROUPS - 1)]
        pltpu.make_async_copy(some, some, recv_sem.at[k]).wait()

    def sent(box, k):
        some = box.at[pl.ds(0, GROUPS - 1)]
        pltpu.make_async_copy(some, some, send_sem.at[k]).wait()

    def halo_copies(step):
        low_x, high_x = state.at[pl.ds(0, NY)], state.at[pl.ds(CELLS - NY, NY)]
        low_y, high_y = yface.at[step, 0], yface.at[step, 1]
        plan = [
            (gx > 0, low_x, xhalo.at[step, 1], 1, (gx - 1, gy)),
            (gx < 15, high_x, xhalo.at[step, 0], 0, (gx + 1, gy)),
            (gy > 0, low_y, yhalo.at[step, 1], 3, (gx, gy - 1)),
            (gy < 7, high_y, yhalo.at[step, 0], 2, (gx, gy + 1)),
        ]
        return [
            (
                there,
                pltpu.make_async_remote_copy(
                    source,
                    target,
                    halo_send.at[step, side],
                    halo_recv.at[step, side],
                    device_id=device,
                    device_id_type=MESH,
                ),
            )
            for there, source, target, side, device in plan
        ]

    def halo_faces(step):
        def face(i, carry):
            yface[step, 0, pl.ds(i, 1), :] = state[pl.ds(i * NY, 1), :]
            yface[step, 1, pl.ds(i, 1), :] = state[pl.ds(i * NY + NY - 1, 1), :]
            return carry

        lax.fori_loop(0, NX, face, 0, unroll=8)

    def halo_start(step):
        for there, copy in halo_copies(step):

            @pl.when(there)
            def _():
                copy.start()

    def halo_wait(step):
        for there, copy in halo_copies(step):

            @pl.when(there)
            def _():
                copy.wait_send()

        for there, side in ((gx > 0, 0), (gx < 15, 1), (gy > 0, 2), (gy < 7, 3)):
            halo = xhalo.at[step, side] if side < 2 else yhalo.at[step, side - 2]

            @pl.when(there)
            def _():
                pltpu.make_async_copy(halo, halo, halo_recv.at[step, side]).wait()

    def stencil(step, start, stop):
        size = 16
        row = iota((size, NZ), 0)
        last = NY // size - 1

        def slab(i, below, above):
            for b in range(last + 1):
                o = pl.multiple_of(i * NY + b * size, size)
                here = pl.ds(o, size)
                c = state[here, :]
                if b > 0:
                    ym = state[pl.ds(o - 1, size), :]
                else:
                    ym = jnp.where(row == 0, yhalo[step, 0, pl.ds(i, 1), :], pltpu.roll(c, 1, 0))
                if b < last:
                    yp = state[pl.ds(o + 1, size), :]
                else:
                    edge = yhalo[step, 1, pl.ds(i, 1), :]
                    yp = jnp.where(row == size - 1, edge, pltpu.roll(c, size - 1, 0))
                after[here, :] = rate_of(
                    c,
                    below(b * size, size),
                    above(b * size, size),
                    ym,
                    yp,
                    [flux[d, here, :].astype(F32) for d in range(3)],
                    [mix[d, here, :].astype(F32) for d in range(2)],
                )

        def at(i):
            return lambda r, n: state[pl.ds(pl.multiple_of(i * NY + r, 16), n), :]

        def halo(side):
            return lambda r, n: xhalo[step, side, r : r + n, :]

        def inner(i, carry):
            slab(i, at(i - 1), at(i + 1))
            return carry

        if start == 0:
            slab(0, halo(0), at(1))
        lax.fori_loop(max(start, 1), min(stop, NX - 1), inner, 0, unroll=7)
        if stop == NX:
            slab(NX - 1, at(NX - 2), halo(1))

    def gather(source, target):
        def group(o, carry):
            for c in range(CAP):
                target[pl.ds(c * 128 + o, 1), :] = source[pl.ds(site[c, o], 1), :]
            return carry

        lax.fori_loop(0, GROUPS, group, 0, unroll=4)

    def solve(last):
        loops = dot(lookup_mat[...], rhs[...]).astype(BF16)
        for g in range(4):
            rows = slice(g * 256, g * 256 + 256)
            two = dot(blocks[0, rows, :], loops[rows])
            small = dot(blocks[1, rows, :], loops[rows, 0:128])
            rates = two[:, 0:128] + two[:, 128:256] + small
            if last:
                heat[rows, :] = rates
            hi, lo = parts_of(rates)
            rhs[rows, 0:128] = hi
            rhs[rows, 128:256] = lo

    def product(matrix):
        two = dot(matrix[...], rhs[...])
        return lambda c: two[block(c), 0:128] + two[block(c), 128:256]

    for edge, halo, side in ((gx == 0, xhalo, 0), (gx == 15, xhalo, 1), (gy == 0, yhalo, 0), (gy == 7, yhalo, 1)):

        @pl.when(edge)
        def _():
            halo[:, side] = jnp.zeros_like(halo[:, side])

    table = jnp.zeros((128, 128), F32)
    for c in range(CAP):
        first, stop = tall(first_ref[c : c + 1, :]), tall(stop_ref[c : c + 1, :])
        table = jnp.where(lane == c, first, table)
        first, stop = first.astype(jnp.int32), stop.astype(jnp.int32)
        masks[block(c), :] = jnp.where((lane >= first) & (lane < stop), 1.0, 0.0)
        indices(c, first, pack_own, unpack_own)
    out_one[:, 4, :] = table
    loads[0].wait()
    gather(state, base)
    pack(lambda c: base[block(c), :] * masks[block(c), :], pack_own, out_one)
    halo_faces(0)

    lookup = lookup_row[...]
    lookup = jnp.where(lookup < SLOTS, (lookup & 7) * 128 + lax.shift_right_logical(lookup, 3), SLOTS)

    def build(o, carry):
        rows = pl.ds(pl.multiple_of(o * 128, 128), 128)
        return_mat[rows, :] = one_hot(lookup == iota((128, SLOTS), 0) + o * 128)
        return carry

    lax.fori_loop(0, 8, build, 0)
    pl.semaphore_wait(barrier, GROUPS - 1)
    halo_start(0)
    send(out_one, in_one, 0)

    for o in range(8):
        piece = lookup[:, block(o)]
        column = (tall(lax.shift_right_logical(piece, 3)) * 8.0 + tall(piece & 7)).astype(jnp.int32)
        for c in range(CAP):
            lookup_mat[block(o), block(c)] = one_hot(column == lane + c * 128)
    loads[3].wait()
    tile = one_hot(iota((32, 256), 1) % 32 == iota((32, 256), 0))
    own_block = (iota((SLOTS, 256), 0) // 32) % 8 == iota((SLOTS, 256), 1) // 32
    for part, piece in enumerate(parts_of(solver[...])):
        blocks[part] = jnp.where(own_block, dot(piece, tile), 0.0).astype(BF16)

    loads[1].wait()
    loads[2].wait()
    halo_wait(0)
    stencil(0, 0, 64)
    receive(in_one, 0)
    sources = in_one[:, 4, :]
    for c in range(CAP):
        first = dot(jnp.where(lane == c, sources, 0.0).astype(BF16), jnp.ones((128, 128), BF16))
        indices(c, first.astype(jnp.int32), pack_got, unpack_got)
    unpack(in_one, unpack_got, got)
    solve(False)
    pack(product(return_mat), pack_got, out_box.at[0])
    send(out_box.at[0], in_box.at[0], 1)

    stencil(0, 64, 128)
    gather(after, base)
    for o in range(CAP):
        piece = site_ref[o : o + 1, :]
        column = (tall(lax.shift_right_logical(piece, 6)) * 64.0 + tall(piece & 63)).astype(jnp.int32)
        for q in range(CAP):
            cell_mat[block(o), block(q)] = one_hot(column == site_ref[q : q + 1, :])
    for q in range(CAP):
        row_hot[:, block(q)] = one_hot((site_ref[q : q + 1, :] & 63) == iota((NY, 128), 0))

    receive(in_box.at[0], 1)
    unpack(in_box.at[0], unpack_own, own)
    deposit = product(cell_mat)
    pack(lambda c: (base[block(c), :] - deposit(c)) * masks[block(c), :], pack_own, out_box.at[1])
    send(out_box.at[1], in_box.at[1], 2)

    def picks(o, target):
        for i in range(16):
            for q in range(CAP):
                there = lax.shift_right_logical(site_ref[q : q + 1, :], 6) == o * 16 + i
                there = one_hot(jnp.broadcast_to(there, (16, 128)))
                for r in range(NY // 16):
                    rows = slice(r * 16, r * 16 + 16)
                    target[i * NY + r * 16 : i * NY + r * 16 + 16, block(q)] = row_hot[rows, block(q)] * there

    def lay(o, source):
        rows = pl.ds(pl.multiple_of(o * 1024, 1024), 1024)
        two = dot(source[...], rhs[...])
        state[rows, :] = after[rows, :] - (two[:, 0:128] + two[:, 128:256])

    def two_blocks(o, carry):
        picks(2 * o + 1, pick_b)
        lay(2 * o, pick_a)
        picks(2 * o + 2, pick_a)
        lay(2 * o + 1, pick_b)
        return carry

    picks(0, pick_a)
    lax.fori_loop(0, 4, two_blocks, 0)
    halo_faces(1)
    halo_start(1)
    receive(in_box.at[1], 2)
    unpack(in_box.at[1], unpack_got, got)
    solve(True)
    pack(product(return_mat), pack_got, out_box.at[2])
    send(out_box.at[2], in_box.at[2], 3)
    store_heat = pltpu.make_async_copy(heat, heat_out, store_sem.at[1])
    store_heat.start()

    halo_wait(1)
    stencil(1, 0, 128)
    store = pltpu.make_async_copy(after, grid_out, store_sem.at[0])
    store.start()
    gather(after, base)
    receive(in_box.at[2], 3)
    unpack(in_box.at[2], unpack_own, own)
    deposit = product(cell_mat)
    for c in range(CAP):
        columns_out[block(c), :] = base[block(c), :] - deposit(c)
    sent(out_one, 0)
    for k in range(3):
        sent(out_box.at[k], k + 1)
    store_heat.wait()
    store.wait()


def settle(site, grid_hbm, rows_hbm, heat_hbm, out_hbm, heat_out, held, rows_ref, heat_ref, sem):
    load = pltpu.make_async_copy(grid_hbm, held, sem.at[0])
    rows = pltpu.make_async_copy(rows_hbm, rows_ref, sem.at[1])
    heat = pltpu.make_async_copy(heat_hbm, heat_ref, sem.at[2])
    load.start()
    rows.start()
    heat.start()
    heat.wait()
    heat = pltpu.make_async_copy(heat_ref, heat_out, sem.at[2])
    heat.start()
    rows.wait()
    load.wait()

    def group(o, carry):
        for c in range(CAP):
            held[pl.ds(site[c, o], 1), :] = rows_ref[pl.ds(c * 128 + o, 1), :]
        return carry

    lax.fori_loop(0, GROUPS, group, 0, unroll=4)
    store = pltpu.make_async_copy(held, out_hbm, sem.at[3])
    store.start()
    store.wait()
    heat.wait()


VMEM = pl.BlockSpec(memory_space=pltpu.VMEM)
SMEM = pl.BlockSpec(memory_space=pltpu.SMEM)
ANY = pl.BlockSpec(memory_space=pl.ANY)


def local(u, flux, mix, site, first, stop, lookup, order, solver):
    def flat(table):
        return jnp.swapaxes(table.reshape(GROUPS, CAP), 0, 1)

    slots = flat(site)
    grid_shape = jax.ShapeDtypeStruct((CELLS, NZ), F32)
    slot_shape = jax.ShapeDtypeStruct((SLOTS, NZ), F32)
    slot_f32 = pltpu.VMEM((SLOTS, NZ), F32)
    slot_i32 = pltpu.VMEM((SLOTS, NZ), jnp.int32)
    square = pltpu.VMEM((SLOTS, SLOTS), BF16)
    grid, rows, heat = pl.pallas_call(
        transport,
        out_shape=(grid_shape, slot_shape, slot_shape),
        in_specs=[SMEM, ANY, ANY, ANY] + [VMEM] * 4 + [ANY],
        out_specs=(ANY, VMEM, ANY),
        scratch_shapes=[
            pltpu.VMEM((CELLS, NZ), F32),
            pltpu.VMEM((CELLS, NZ), F32),
            pltpu.VMEM((3, CELLS, NZ), BF16),
            pltpu.VMEM((2, CELLS, NZ), BF16),
            pltpu.VMEM((2, 2, NY, NZ), F32),
            pltpu.VMEM((2, 2, NX, NZ), F32),
            pltpu.VMEM((2, 2, NX, NZ), F32),
            slot_f32,
            slot_f32,
            slot_i32,
            slot_i32,
            slot_i32,
            slot_i32,
            square,
            square,
            square,
            pltpu.VMEM((SLOTS, 32), F32),
            pltpu.VMEM((2, SLOTS, 256), BF16),
            pltpu.VMEM((SLOTS, 256), BF16),
            slot_f32,
            pltpu.VMEM((NY, SLOTS), BF16),
            square,
            square,
            pltpu.VMEM((3, GROUPS, 4, NZ), F32),
            pltpu.VMEM((3, GROUPS, 4, NZ), F32),
            pltpu.VMEM((GROUPS, 5, NZ), F32),
            pltpu.VMEM((GROUPS, 5, NZ), F32),
            pltpu.SemaphoreType.DMA((4,)),
            pltpu.SemaphoreType.DMA((2,)),
            pltpu.SemaphoreType.DMA((2, 4)),
            pltpu.SemaphoreType.DMA((2, 4)),
            pltpu.SemaphoreType.DMA((4,)),
            pltpu.SemaphoreType.DMA((4,)),
        ],
        compiler_params=pltpu.CompilerParams(
            collective_id=0, has_side_effects=True, vmem_limit_bytes=60 << 20
        ),
    )(
        slots,
        u.reshape(CELLS, NZ),
        flux.reshape(3, CELLS, NZ),
        mix.reshape(2, CELLS, NZ),
        flat(first),
        flat(stop),
        slots,
        lookup.reshape(1, SLOTS),
        solver.reshape(SLOTS, 32),
    )
    grid, heat = pl.pallas_call(
        settle,
        out_shape=(grid_shape, slot_shape),
        in_specs=[SMEM, ANY, ANY, ANY],
        out_specs=(ANY, ANY),
        scratch_shapes=[pltpu.VMEM((CELLS, NZ), F32), slot_f32, slot_f32, pltpu.SemaphoreType.DMA((4,))],
        compiler_params=pltpu.CompilerParams(vmem_limit_bytes=60 << 20),
    )(slots, grid, rows, heat)
    return grid.reshape(NX, NY, NZ), heat.reshape(1, 1, SLOTS, NZ)


def solution(mesh):
    placed = (
        P("gx", "gy", None),
        P(None, "gx", "gy", None),
        P(None, "gx", "gy", None),
        P("gx", "gy", None, None),
        P("gx", "gy", None, None),
        P("gx", "gy", None, None),
        P("gx", "gy", None),
        P("gx", "gy", None),
        P("gx", "gy", None, None, None),
    )
    return jax.shard_map(
        local,
        mesh=mesh,
        in_specs=placed,
        out_specs=(P("gx", "gy", None), P("gx", "gy", None, None)),
        check_vma=False,
    )
```

```python
import functools

import jax
import jax.numpy as jnp
from jax import lax
from jax.experimental import pallas as pl
from jax.experimental.pallas import tpu as pltpu
from jax.sharding import PartitionSpec as P

MESH = pl.DeviceIdType.MESH
F32 = jnp.float32
BF16 = jnp.bfloat16

NX, NY, NZ = 128, 64, 128
CELLS = NX * NY
GROUPS, CAP = 128, 8
SLOTS = GROUPS * CAP
HALF = 64

HOPS = (0, 1, 2, 1)
OFFSETS = sorted(
    [(a, b, c, d) for a in range(4) for b in range(4) for c in range(4) for d in range(2)][1:],
    key=lambda o: -(HOPS[o[0]] + HOPS[o[1]] + HOPS[o[2]] + 0.3 * o[3]),
)


def iota(shape, dim):
    return lax.broadcasted_iota(jnp.int32, shape, dim)


def dot(a, b):
    return jnp.dot(a, b, preferred_element_type=F32)


def parts_of(x):
    hi = x.astype(BF16)
    return hi, (x - hi.astype(F32)).astype(BF16)


def one_hot(mask):
    return jnp.where(mask, 1.0, 0.0).astype(BF16)


def tall(row):
    eye = iota((128, 128), 0) == iota((128, 128), 1)
    spread = jnp.where(eye, row.astype(F32), 0.0).astype(BF16)
    return dot(spread, jnp.ones((128, 128), BF16))


def rate_of(c, xm, xp, ym, yp, flux, mix):
    vx, vy, vz = flux
    kh, kv = mix
    lane = iota(c.shape, 1)
    zm = jnp.where(lane == 0, 0.0, pltpu.roll(c, 1, 1))
    zp = jnp.where(lane == NZ - 1, 0.0, pltpu.roll(c, NZ - 1, 1))
    xa, xb, ya, yb, za, zb = xp - c, c - xm, yp - c, c - ym, zp - c, c - zm
    advect = vx * jnp.where(vx > 0.0, xb, xa)
    advect += vy * jnp.where(vy > 0.0, yb, ya)
    advect += vz * jnp.where(vz > 0.0, zb, za)
    return c + 0.1 * (kh * ((xa - xb) + (ya - yb)) + kv * (za - zb) - advect)


def transport(
    u_hbm,
    flux_hbm,
    mix_hbm,
    first_hbm,
    stop_hbm,
    site_hbm,
    lookup_hbm,
    solver_hbm,
    after,
    columns_out,
    heat,
    site,
    first_ref,
    stop_ref,
    site_ref,
    lookup_row,
    state,
    flux,
    mix,
    xhalo,
    yhalo,
    yface,
    base,
    masks,
    pack_own,
    unpack_own,
    pack_got,
    unpack_got,
    lookup_mat,
    return_mat,
    cell_mat,
    solver,
    blocks,
    rhs,
    row_hot,
    pick_a,
    pick_b,
    out_box,
    in_box,
    out_one,
    in_one,
    load_sem,
    halo_send,
    halo_recv,
    send_sem,
    recv_sem,
):
    gx, gy = lax.axis_index("gx"), lax.axis_index("gy")
    me = gx * 8 + gy
    px, py = lax.div(gx, 4), lax.rem(gx, 4)
    pz, pc = lax.div(gy, 2), lax.rem(gy, 2)
    xs = [lax.rem(px + i, 4) for i in range(4)]
    ys = [lax.rem(py + i, 4) for i in range(4)]
    zs = [lax.rem(pz + i, 4) for i in range(4)]
    cs = [lax.rem(pc + i, 2) for i in range(2)]
    peers = [(xs[a] * 4 + ys[b], zs[c] * 2 + cs[d]) for a, b, c, d in OFFSETS]

    moves = (
        (first_hbm, first_ref),
        (stop_hbm, stop_ref),
        (site_hbm, site),
        (u_hbm, state),
        (site_hbm, site_ref),
        (lookup_hbm, lookup_row),
        (solver_hbm, solver),
        (flux_hbm, flux),
        (mix_hbm, mix),
    )
    loads = [
        pltpu.make_async_copy(source, target, load_sem.at[i])
        for i, (source, target) in enumerate(moves)
    ]
    for load in loads:
        load.start()
    barrier = pltpu.get_barrier_semaphore()
    for peer in peers:
        pl.semaphore_signal(barrier, inc=1, device_id=peer, device_id_type=MESH)

    lane = iota((128, 128), 1)

    def block(c):
        return slice(c * 128, c * 128 + 128)

    def indices(c, first, pack_ref, unpack_ref):
        shift = HALF if c >= 4 else 0
        pack_ref[block(c), :] = (lane + first + shift) & 127
        unpack_ref[block(c), :] = (lane - first + shift) & 127

    def pack(value, index, box):
        for r in range(4):
            left, right = (
                jnp.take_along_axis(value(c), index[block(c), :], axis=1) for c in (r, r + 4)
            )
            box[:, r, :] = jnp.where(lane < HALF, left, right)

    def unpack(box, index, keep):
        for r in range(4):
            pair = box[:, r, :]
            for c in (r, r + 4):
                wide = jnp.take_along_axis(pair, index[block(c), :], axis=1)
                hi, lo = parts_of(jnp.where(keep(c), wide, 0.0))
                rhs[block(c), 0:128] = hi
                rhs[block(c), 128:256] = lo

    def own(c):
        return masks[block(c), :] > 0.0

    def got(c):
        return ((unpack_got[block(c), :] - (HALF if c >= 4 else 0)) & 127) < HALF

    def send(box, landing, k):
        for x, y in peers:
            pltpu.make_async_remote_copy(
                box.at[x * 8 + y],
                landing.at[me],
                send_sem.at[k],
                recv_sem.at[k],
                device_id=(x, y),
                device_id_type=MESH,
            ).start()
        landing[me] = box[me]

    def receive(landing, k):
        some = landing.at[pl.ds(0, GROUPS - 1)]
        pltpu.make_async_copy(some, some, recv_sem.at[k]).wait()

    def sent(box, k):
        some = box.at[pl.ds(0, GROUPS - 1)]
        pltpu.make_async_copy(some, some, send_sem.at[k]).wait()

    def halo_copies(step):
        low_x, high_x = state.at[pl.ds(0, NY)], state.at[pl.ds(CELLS - NY, NY)]
        low_y, high_y = yface.at[step, 0], yface.at[step, 1]
        plan = [
            (gx > 0, low_x, xhalo.at[step, 1], 1, (gx - 1, gy)),
            (gx < 15, high_x, xhalo.at[step, 0], 0, (gx + 1, gy)),
            (gy > 0, low_y, yhalo.at[step, 1], 3, (gx, gy - 1)),
            (gy < 7, high_y, yhalo.at[step, 0], 2, (gx, gy + 1)),
        ]
        return [
            (
                there,
                pltpu.make_async_remote_copy(
                    source,
                    target,
                    halo_send.at[step, side],
                    halo_recv.at[step, side],
                    device_id=device,
                    device_id_type=MESH,
                ),
            )
            for there, source, target, side, device in plan
        ]

    def halo_faces(step):
        def face(i, carry):
            yface[step, 0, pl.ds(i, 1), :] = state[pl.ds(i * NY, 1), :]
            yface[step, 1, pl.ds(i, 1), :] = state[pl.ds(i * NY + NY - 1, 1), :]
            return carry

        lax.fori_loop(0, NX, face, 0, unroll=8)

    def halo_start(step):
        for there, copy in halo_copies(step):

            @pl.when(there)
            def _():
                copy.start()

    def halo_wait(step):
        for there, copy in halo_copies(step):

            @pl.when(there)
            def _():
                copy.wait_send()

        for there, side in ((gx > 0, 0), (gx < 15, 1), (gy > 0, 2), (gy < 7, 3)):
            halo = xhalo.at[step, side] if side < 2 else yhalo.at[step, side - 2]

            @pl.when(there)
            def _():
                pltpu.make_async_copy(halo, halo, halo_recv.at[step, side]).wait()

    def stencil(step, start, stop):
        size = 16
        row = iota((size, NZ), 0)
        last = NY // size - 1

        def slab(i, below, above):
            for b in range(last + 1):
                o = pl.multiple_of(i * NY + b * size, size)
                here = pl.ds(o, size)
                c = state[here, :]
                if b > 0:
                    ym = state[pl.ds(o - 1, size), :]
                else:
                    ym = jnp.where(row == 0, yhalo[step, 0, pl.ds(i, 1), :], pltpu.roll(c, 1, 0))
                if b < last:
                    yp = state[pl.ds(o + 1, size), :]
                else:
                    edge = yhalo[step, 1, pl.ds(i, 1), :]
                    yp = jnp.where(row == size - 1, edge, pltpu.roll(c, size - 1, 0))
                after[here, :] = rate_of(
                    c,
                    below(b * size, size),
                    above(b * size, size),
                    ym,
                    yp,
                    [flux[d, here, :].astype(F32) for d in range(3)],
                    [mix[d, here, :].astype(F32) for d in range(2)],
                )

        def at(i):
            return lambda r, n: state[pl.ds(pl.multiple_of(i * NY + r, 16), n), :]

        def halo(side):
            return lambda r, n: xhalo[step, side, r : r + n, :]

        def inner(i, carry):
            slab(i, at(i - 1), at(i + 1))
            return carry

        if start == 0:
            slab(0, halo(0), at(1))
        lax.fori_loop(max(start, 1), min(stop, NX - 1), inner, 0, unroll=7)
        if stop == NX:
            slab(NX - 1, at(NX - 2), halo(1))

    def gather(source, target):
        def group(o, carry):
            for c in range(CAP):
                target[pl.ds(c * 128 + o, 1), :] = source[pl.ds(site[c, o], 1), :]
            return carry

        lax.fori_loop(0, GROUPS, group, 0, unroll=4)

    def solve(last):
        loops = dot(lookup_mat[...], rhs[...]).astype(BF16)
        for g in range(4):
            rows = slice(g * 256, g * 256 + 256)
            two = dot(blocks[0, rows, :], loops[rows])
            small = dot(blocks[1, rows, :], loops[rows, 0:128])
            rates = two[:, 0:128] + two[:, 128:256] + small
            if last:
                heat[rows, :] = rates
            hi, lo = parts_of(rates)
            rhs[rows, 0:128] = hi
            rhs[rows, 128:256] = lo

    def product(matrix):
        two = dot(matrix[...], rhs[...])
        return lambda c: two[block(c), 0:128] + two[block(c), 128:256]

    for edge, halo, side in ((gx == 0, xhalo, 0), (gx == 15, xhalo, 1), (gy == 0, yhalo, 0), (gy == 7, yhalo, 1)):

        @pl.when(edge)
        def _():
            halo[:, side] = jnp.zeros_like(halo[:, side])

    loads[0].wait()
    loads[1].wait()
    table = jnp.zeros((128, 128), F32)
    for c in range(CAP):
        first, stop = tall(first_ref[c : c + 1, :]), tall(stop_ref[c : c + 1, :])
        table = jnp.where(lane == c, first, table)
        first, stop = first.astype(jnp.int32), stop.astype(jnp.int32)
        masks[block(c), :] = jnp.where((lane >= first) & (lane < stop), 1.0, 0.0)
        indices(c, first, pack_own, unpack_own)
    out_one[:, 4, :] = table
    loads[2].wait()
    loads[3].wait()
    gather(state, base)
    pack(lambda c: base[block(c), :] * masks[block(c), :], pack_own, out_one)
    halo_faces(0)

    loads[5].wait()
    lookup = lookup_row[...]
    lookup = jnp.where(lookup < SLOTS, (lookup & 7) * 128 + lax.shift_right_logical(lookup, 3), SLOTS)

    def build(o, carry):
        rows = pl.ds(pl.multiple_of(o * 128, 128), 128)
        return_mat[rows, :] = one_hot(lookup == iota((128, SLOTS), 0) + o * 128)
        return carry

    lax.fori_loop(0, 8, build, 0)
    for o in range(8):
        piece = lookup[:, block(o)]
        column = (tall(lax.shift_right_logical(piece, 3)) * 8.0 + tall(piece & 7)).astype(jnp.int32)
        for c in range(CAP):
            lookup_mat[block(o), block(c)] = one_hot(column == lane + c * 128)
    loads[6].wait()
    tile = one_hot(iota((32, 256), 1) % 32 == iota((32, 256), 0))
    own_block = (iota((SLOTS, 256), 0) // 32) % 8 == iota((SLOTS, 256), 1) // 32
    for part, piece in enumerate(parts_of(solver[...])):
        blocks[part] = jnp.where(own_block, dot(piece, tile), 0.0).astype(BF16)

    pl.semaphore_wait(barrier, GROUPS - 1)
    halo_start(0)
    send(out_one, in_one, 0)

    for load in (loads[4], loads[7], loads[8]):
        load.wait()
    halo_wait(0)
    stencil(0, 0, 64)
    receive(in_one, 0)
    sources = in_one[:, 4, :]
    for c in range(CAP):
        first = dot(jnp.where(lane == c, sources, 0.0).astype(BF16), jnp.ones((128, 128), BF16))
        indices(c, first.astype(jnp.int32), pack_got, unpack_got)
    unpack(in_one, unpack_got, got)
    solve(False)
    pack(product(return_mat), pack_got, out_box.at[0])
    send(out_box.at[0], in_box.at[0], 1)

    stencil(0, 64, 128)
    gather(after, base)
    for o in range(CAP):
        piece = site_ref[o : o + 1, :]
        column = (tall(lax.shift_right_logical(piece, 6)) * 64.0 + tall(piece & 63)).astype(jnp.int32)
        for q in range(CAP):
            cell_mat[block(o), block(q)] = one_hot(column == site_ref[q : q + 1, :])
    for q in range(CAP):
        row_hot[:, block(q)] = one_hot((site_ref[q : q + 1, :] & 63) == iota((NY, 128), 0))

    receive(in_box.at[0], 1)
    unpack(in_box.at[0], unpack_own, own)
    deposit = product(cell_mat)
    pack(lambda c: (base[block(c), :] - deposit(c)) * masks[block(c), :], pack_own, out_box.at[1])
    send(out_box.at[1], in_box.at[1], 2)

    def picks(o, target):
        for i in range(16):
            for q in range(CAP):
                there = lax.shift_right_logical(site_ref[q : q + 1, :], 6) == o * 16 + i
                there = one_hot(jnp.broadcast_to(there, (16, 128)))
                for r in range(NY // 16):
                    rows = slice(r * 16, r * 16 + 16)
                    target[i * NY + r * 16 : i * NY + r * 16 + 16, block(q)] = row_hot[rows, block(q)] * there

    def lay(o, source):
        rows = pl.ds(pl.multiple_of(o * 1024, 1024), 1024)
        two = dot(source[...], rhs[...])
        state[rows, :] = after[rows, :] - (two[:, 0:128] + two[:, 128:256])

    def two_blocks(o, carry):
        picks(2 * o + 1, pick_b)
        lay(2 * o, pick_a)
        picks(2 * o + 2, pick_a)
        lay(2 * o + 1, pick_b)
        return carry

    picks(0, pick_a)
    lax.fori_loop(0, 4, two_blocks, 0)
    halo_faces(1)
    halo_start(1)
    receive(in_box.at[1], 2)
    unpack(in_box.at[1], unpack_got, got)
    solve(True)
    pack(product(return_mat), pack_got, out_box.at[2])
    send(out_box.at[2], in_box.at[2], 3)

    halo_wait(1)
    stencil(1, 0, 128)
    gather(after, base)
    receive(in_box.at[2], 3)
    unpack(in_box.at[2], unpack_own, own)
    deposit = product(cell_mat)
    for c in range(CAP):
        columns_out[block(c), :] = base[block(c), :] - deposit(c)
    sent(out_one, 0)
    for k in range(3):
        sent(out_box.at[k], k + 1)


def settle(site, grid, rows, heat, out_hbm, heat_out, changed, sem):
    store_heat = pltpu.make_async_copy(heat, heat_out, sem.at[0])
    store_heat.start()

    def group(o, carry):
        for c in range(CAP):
            changed[pl.ds(site[c, o], 1), :] = rows[pl.ds(c * 128 + o, 1), :]
        return carry

    lax.fori_loop(0, GROUPS, group, 0, unroll=4)
    store = pltpu.make_async_copy(changed, out_hbm, sem.at[1])
    store.start()
    store_heat.wait()
    store.wait()


VMEM = pl.BlockSpec(memory_space=pltpu.VMEM)
SMEM = pl.BlockSpec(memory_space=pltpu.SMEM)
ANY = pl.BlockSpec(memory_space=pl.ANY)
HBM = pl.BlockSpec(memory_space=pltpu.HBM)


def local(u, flux, mix, site, first, stop, lookup, order, solver):
    def flat(table):
        return jnp.swapaxes(table.reshape(GROUPS, CAP), 0, 1)

    slots = flat(site)
    grid_shape = jax.ShapeDtypeStruct((CELLS, NZ), F32)
    slot_shape = jax.ShapeDtypeStruct((SLOTS, NZ), F32)
    slot_f32 = pltpu.VMEM((SLOTS, NZ), F32)
    slot_i32 = pltpu.VMEM((SLOTS, NZ), jnp.int32)
    square = pltpu.VMEM((SLOTS, SLOTS), BF16)
    grid, rows, heat = pl.pallas_call(
        transport,
        out_shape=(pltpu.VMEM((CELLS, NZ), F32), pltpu.VMEM((SLOTS, NZ), F32), pltpu.VMEM((SLOTS, NZ), F32)),
        in_specs=[HBM] * 8,
        out_specs=(VMEM, VMEM, VMEM),
        scratch_shapes=[
            pltpu.SMEM((CAP, GROUPS), jnp.int32),
            pltpu.VMEM((CAP, GROUPS), jnp.int32),
            pltpu.VMEM((CAP, GROUPS), jnp.int32),
            pltpu.VMEM((CAP, GROUPS), jnp.int32),
            pltpu.VMEM((1, SLOTS), jnp.int32),
            pltpu.VMEM((CELLS, NZ), F32),
            pltpu.VMEM((3, CELLS, NZ), BF16),
            pltpu.VMEM((2, CELLS, NZ), BF16),
            pltpu.VMEM((2, 2, NY, NZ), F32),
            pltpu.VMEM((2, 2, NX, NZ), F32),
            pltpu.VMEM((2, 2, NX, NZ), F32),
            slot_f32,
            slot_f32,
            slot_i32,
            slot_i32,
            slot_i32,
            slot_i32,
            square,
            square,
            square,
            pltpu.VMEM((SLOTS, 32), F32),
            pltpu.VMEM((2, SLOTS, 256), BF16),
            pltpu.VMEM((SLOTS, 256), BF16),
            pltpu.VMEM((NY, SLOTS), BF16),
            square,
            square,
            pltpu.VMEM((3, GROUPS, 4, NZ), F32),
            pltpu.VMEM((3, GROUPS, 4, NZ), F32),
            pltpu.VMEM((GROUPS, 5, NZ), F32),
            pltpu.VMEM((GROUPS, 5, NZ), F32),
            pltpu.SemaphoreType.DMA((9,)),
            pltpu.SemaphoreType.DMA((2, 4)),
            pltpu.SemaphoreType.DMA((2, 4)),
            pltpu.SemaphoreType.DMA((4,)),
            pltpu.SemaphoreType.DMA((4,)),
        ],
        compiler_params=pltpu.CompilerParams(
            collective_id=0, has_side_effects=True, vmem_limit_bytes=57 << 20
        ),
    )(
        u.reshape(CELLS, NZ),
        flux.reshape(3, CELLS, NZ),
        mix.reshape(2, CELLS, NZ),
        flat(first),
        flat(stop),
        slots,
        lookup.reshape(1, SLOTS),
        solver.reshape(SLOTS, 32),
    )
    grid, heat, _ = pl.pallas_call(
        settle,
        out_shape=(grid_shape, slot_shape, pltpu.VMEM((CELLS, NZ), F32)),
        in_specs=[SMEM, VMEM, VMEM, VMEM],
        out_specs=(ANY, ANY, VMEM),
        scratch_shapes=[pltpu.SemaphoreType.DMA((2,))],
        input_output_aliases={1: 2},
        compiler_params=pltpu.CompilerParams(vmem_limit_bytes=16 << 20),
    )(slots, grid, rows, heat)
    return grid.reshape(NX, NY, NZ), heat.reshape(1, 1, SLOTS, NZ)


def solution(mesh):
    placed = (
        P("gx", "gy", None),
        P(None, "gx", "gy", None),
        P(None, "gx", "gy", None),
        P("gx", "gy", None, None),
        P("gx", "gy", None, None),
        P("gx", "gy", None, None),
        P("gx", "gy", None),
        P("gx", "gy", None),
        P("gx", "gy", None, None, None),
    )
    return jax.shard_map(
        local,
        mesh=mesh,
        in_specs=placed,
        out_specs=(P("gx", "gy", None), P("gx", "gy", None, None)),
        check_vma=False,
    )
```

```python
import functools

import jax
import jax.numpy as jnp
from jax import lax
from jax.experimental import pallas as pl
from jax.experimental.pallas import tpu as pltpu
from jax.sharding import PartitionSpec as P

MESH = pl.DeviceIdType.MESH
F32 = jnp.float32
BF16 = jnp.bfloat16

NX, NY, NZ = 128, 64, 128
CELLS = NX * NY
GROUPS, CAP = 128, 8
SLOTS = GROUPS * CAP
HALF = 64

HOPS = (0, 1, 2, 1)
OFFSETS = sorted(
    [(a, b, c, d) for a in range(4) for b in range(4) for c in range(4) for d in range(2)][1:],
    key=lambda o: -(HOPS[o[0]] + HOPS[o[1]] + HOPS[o[2]] + 0.3 * o[3]),
)


def iota(shape, dim):
    return lax.broadcasted_iota(jnp.int32, shape, dim)


def dot(a, b):
    return jnp.dot(a, b, preferred_element_type=F32)


def parts_of(x):
    hi = x.astype(BF16)
    return hi, (x - hi.astype(F32)).astype(BF16)


def one_hot(mask):
    return jnp.where(mask, 1.0, 0.0).astype(BF16)


def tall(row):
    eye = iota((128, 128), 0) == iota((128, 128), 1)
    spread = jnp.where(eye, row.astype(F32), 0.0).astype(BF16)
    return dot(spread, jnp.ones((128, 128), BF16))


def rate_of(c, xm, xp, ym, yp, flux, mix):
    vx, vy, vz = flux
    kh, kv = mix
    lane = iota(c.shape, 1)
    zm = jnp.where(lane == 0, 0.0, pltpu.roll(c, 1, 1))
    zp = jnp.where(lane == NZ - 1, 0.0, pltpu.roll(c, NZ - 1, 1))
    xa, xb, ya, yb, za, zb = xp - c, c - xm, yp - c, c - ym, zp - c, c - zm
    advect = vx * jnp.where(vx > 0.0, xb, xa)
    advect += vy * jnp.where(vy > 0.0, yb, ya)
    advect += vz * jnp.where(vz > 0.0, zb, za)
    return c + 0.1 * (kh * ((xa - xb) + (ya - yb)) + kv * (za - zb) - advect)


def transport(
    u_hbm,
    flux_hbm,
    mix_hbm,
    first_hbm,
    stop_hbm,
    site_hbm,
    lookup_hbm,
    solver_hbm,
    after,
    columns_out,
    heat,
    site,
    first_ref,
    stop_ref,
    site_ref,
    lookup_row,
    state,
    flux,
    mix,
    xhalo,
    yhalo,
    yface,
    base,
    masks,
    pack_own,
    unpack_own,
    pack_got,
    unpack_got,
    lookup_mat,
    return_mat,
    cell_mat,
    solver,
    blocks,
    rhs,
    row_hot,
    pick_a,
    pick_b,
    out_box,
    in_box,
    out_one,
    in_one,
    load_sem,
    halo_send,
    halo_recv,
    send_sem,
    recv_sem,
):
    gx, gy = lax.axis_index("gx"), lax.axis_index("gy")
    me = gx * 8 + gy
    px, py = lax.div(gx, 4), lax.rem(gx, 4)
    pz, pc = lax.div(gy, 2), lax.rem(gy, 2)
    xs = [lax.rem(px + i, 4) for i in range(4)]
    ys = [lax.rem(py + i, 4) for i in range(4)]
    zs = [lax.rem(pz + i, 4) for i in range(4)]
    cs = [lax.rem(pc + i, 2) for i in range(2)]
    peers = [(xs[a] * 4 + ys[b], zs[c] * 2 + cs[d]) for a, b, c, d in OFFSETS]

    moves = (
        (first_hbm, first_ref),
        (stop_hbm, stop_ref),
        (site_hbm, site),
        (u_hbm, state),
        (site_hbm, site_ref),
        (lookup_hbm, lookup_row),
        (solver_hbm, solver),
        (flux_hbm, flux),
        (mix_hbm, mix),
    )
    loads = [
        pltpu.make_async_copy(source, target, load_sem.at[i])
        for i, (source, target) in enumerate(moves)
    ]
    for load in loads:
        load.start()
    barrier = pltpu.get_barrier_semaphore()
    for peer in peers:
        pl.semaphore_signal(barrier, inc=1, device_id=peer, device_id_type=MESH)

    lane = iota((128, 128), 1)

    def block(c):
        return slice(c * 128, c * 128 + 128)

    def indices(c, first, pack_ref, unpack_ref):
        shift = HALF if c >= 4 else 0
        pack_ref[block(c), :] = (lane + first + shift) & 127
        if unpack_ref is not None:
            unpack_ref[block(c), :] = (lane - first + shift) & 127

    def pack(value, index, box):
        for r in range(4):
            left, right = (
                jnp.take_along_axis(value(c), index[block(c), :], axis=1) for c in (r, r + 4)
            )
            box[:, r, :] = jnp.where(lane < HALF, left, right)

    def unpack(box, index, keep):
        for r in range(4):
            pair = box[:, r, :]
            for c in (r, r + 4):
                wide = jnp.take_along_axis(pair, index[block(c), :], axis=1)
                hi, lo = parts_of(jnp.where(keep(c), wide, 0.0))
                rhs[block(c), 0:128] = hi
                rhs[block(c), 128:256] = lo

    def own(c):
        return masks[block(c), :] > 0.0

    def got(c):
        return ((unpack_got[block(c), :] - (HALF if c >= 4 else 0)) & 127) < HALF

    def send(box, landing, k):
        for x, y in peers:
            pltpu.make_async_remote_copy(
                box.at[x * 8 + y],
                landing.at[me],
                send_sem.at[k],
                recv_sem.at[k],
                device_id=(x, y),
                device_id_type=MESH,
            ).start()
        landing[me] = box[me]

    def receive(landing, k):
        some = landing.at[pl.ds(0, GROUPS - 1)]
        pltpu.make_async_copy(some, some, recv_sem.at[k]).wait()

    def sent(box, k):
        some = box.at[pl.ds(0, GROUPS - 1)]
        pltpu.make_async_copy(some, some, send_sem.at[k]).wait()

    def halo_copies(step):
        low_x, high_x = state.at[pl.ds(0, NY)], state.at[pl.ds(CELLS - NY, NY)]
        low_y, high_y = yface.at[step, 0], yface.at[step, 1]
        plan = [
            (gx > 0, low_x, xhalo.at[step, 1], 1, (gx - 1, gy)),
            (gx < 15, high_x, xhalo.at[step, 0], 0, (gx + 1, gy)),
            (gy > 0, low_y, yhalo.at[step, 1], 3, (gx, gy - 1)),
            (gy < 7, high_y, yhalo.at[step, 0], 2, (gx, gy + 1)),
        ]
        return [
            (
                there,
                pltpu.make_async_remote_copy(
                    source,
                    target,
                    halo_send.at[step, side],
                    halo_recv.at[step, side],
                    device_id=device,
                    device_id_type=MESH,
                ),
            )
            for there, source, target, side, device in plan
        ]

    def halo_faces(step):
        def face(i, carry):
            yface[step, 0, pl.ds(i, 1), :] = state[pl.ds(i * NY, 1), :]
            yface[step, 1, pl.ds(i, 1), :] = state[pl.ds(i * NY + NY - 1, 1), :]
            return carry

        lax.fori_loop(0, NX, face, 0, unroll=8)

    def halo_start(step):
        for there, copy in halo_copies(step):

            @pl.when(there)
            def _():
                copy.start()

    def halo_wait(step):
        for there, copy in halo_copies(step):

            @pl.when(there)
            def _():
                copy.wait_send()

        for there, side in ((gx > 0, 0), (gx < 15, 1), (gy > 0, 2), (gy < 7, 3)):
            halo = xhalo.at[step, side] if side < 2 else yhalo.at[step, side - 2]

            @pl.when(there)
            def _():
                pltpu.make_async_copy(halo, halo, halo_recv.at[step, side]).wait()

    def stencil(step, start, stop):
        size = 16
        row = iota((size, NZ), 0)
        last = NY // size - 1

        def slab(i, below, above):
            for b in range(last + 1):
                o = pl.multiple_of(i * NY + b * size, size)
                here = pl.ds(o, size)
                c = state[here, :]
                if b > 0:
                    ym = state[pl.ds(o - 1, size), :]
                else:
                    ym = jnp.where(row == 0, yhalo[step, 0, pl.ds(i, 1), :], pltpu.roll(c, 1, 0))
                if b < last:
                    yp = state[pl.ds(o + 1, size), :]
                else:
                    edge = yhalo[step, 1, pl.ds(i, 1), :]
                    yp = jnp.where(row == size - 1, edge, pltpu.roll(c, size - 1, 0))
                after[here, :] = rate_of(
                    c,
                    below(b * size, size),
                    above(b * size, size),
                    ym,
                    yp,
                    [flux[d, here, :].astype(F32) for d in range(3)],
                    [mix[d, here, :].astype(F32) for d in range(2)],
                )

        def at(i):
            return lambda r, n: state[pl.ds(pl.multiple_of(i * NY + r, 16), n), :]

        def halo(side):
            return lambda r, n: xhalo[step, side, r : r + n, :]

        def inner(i, carry):
            slab(i, at(i - 1), at(i + 1))
            return carry

        if start == 0:
            slab(0, halo(0), at(1))
        lax.fori_loop(max(start, 1), min(stop, NX - 1), inner, 0, unroll=7)
        if stop == NX:
            slab(NX - 1, at(NX - 2), halo(1))

    def gather(source, target):
        def group(o, carry):
            for c in range(CAP):
                target[pl.ds(c * 128 + o, 1), :] = source[pl.ds(site[c, o], 1), :]
            return carry

        lax.fori_loop(0, GROUPS, group, 0, unroll=4)

    def solve(last):
        loops = dot(lookup_mat[...], rhs[...]).astype(BF16)
        for g in range(4):
            rows = slice(g * 256, g * 256 + 256)
            two = dot(blocks[0, rows, :], loops[rows])
            small = dot(blocks[1, rows, :], loops[rows, 0:128])
            rates = two[:, 0:128] + two[:, 128:256] + small
            if last:
                heat[rows, :] = rates
            hi, lo = parts_of(rates)
            rhs[rows, 0:128] = hi
            rhs[rows, 128:256] = lo

    def product(matrix):
        two = dot(matrix[...], rhs[...])
        return lambda c: two[block(c), 0:128] + two[block(c), 128:256]

    for edge, halo, side in ((gx == 0, xhalo, 0), (gx == 15, xhalo, 1), (gy == 0, yhalo, 0), (gy == 7, yhalo, 1)):

        @pl.when(edge)
        def _():
            halo[:, side] = jnp.zeros_like(halo[:, side])

    loads[0].wait()
    loads[1].wait()
    table = jnp.zeros((128, 128), F32)
    for c in range(CAP):
        first, stop = tall(first_ref[c : c + 1, :]), tall(stop_ref[c : c + 1, :])
        table = jnp.where(lane == c, first, table)
        first, stop = first.astype(jnp.int32), stop.astype(jnp.int32)
        masks[block(c), :] = jnp.where((lane >= first) & (lane < stop), 1.0, 0.0)
        indices(c, first, pack_own, None)
    out_one[:, 4, :] = table
    loads[2].wait()
    loads[3].wait()
    gather(state, base)
    pack(lambda c: base[block(c), :] * masks[block(c), :], pack_own, out_one)
    halo_faces(0)

    pl.semaphore_wait(barrier, GROUPS - 1)
    halo_start(0)
    send(out_one, in_one, 0)

    for c in range(CAP):
        unpack_own[block(c), :] = (2 * lane - pack_own[block(c), :]) & 127

    loads[5].wait()
    lookup = lookup_row[...]
    lookup = jnp.where(lookup < SLOTS, (lookup & 7) * 128 + lax.shift_right_logical(lookup, 3), SLOTS)

    def build(o, carry):
        rows = pl.ds(pl.multiple_of(o * 128, 128), 128)
        return_mat[rows, :] = one_hot(lookup == iota((128, SLOTS), 0) + o * 128)
        return carry

    lax.fori_loop(0, 8, build, 0)
    for o in range(8):
        piece = lookup[:, block(o)]
        column = (tall(lax.shift_right_logical(piece, 3)) * 8.0 + tall(piece & 7)).astype(jnp.int32)
        for c in range(CAP):
            lookup_mat[block(o), block(c)] = one_hot(column == lane + c * 128)
    loads[6].wait()
    tile = one_hot(iota((32, 256), 1) % 32 == iota((32, 256), 0))
    own_block = (iota((SLOTS, 256), 0) // 32) % 8 == iota((SLOTS, 256), 1) // 32
    for part, piece in enumerate(parts_of(solver[...])):
        blocks[part] = jnp.where(own_block, dot(piece, tile), 0.0).astype(BF16)

    for load in (loads[4], loads[7], loads[8]):
        load.wait()
    halo_wait(0)
    stencil(0, 0, 64)
    receive(in_one, 0)
    sources = in_one[:, 4, :]
    for c in range(CAP):
        first = dot(jnp.where(lane == c, sources, 0.0).astype(BF16), jnp.ones((128, 128), BF16))
        indices(c, first.astype(jnp.int32), pack_got, unpack_got)
    unpack(in_one, unpack_got, got)
    solve(False)
    pack(product(return_mat), pack_got, out_box.at[0])
    send(out_box.at[0], in_box.at[0], 1)

    stencil(0, 64, 128)
    gather(after, base)
    for o in range(CAP):
        piece = site_ref[o : o + 1, :]
        column = (tall(lax.shift_right_logical(piece, 6)) * 64.0 + tall(piece & 63)).astype(jnp.int32)
        for q in range(CAP):
            cell_mat[block(o), block(q)] = one_hot(column == site_ref[q : q + 1, :])
    for q in range(CAP):
        row_hot[:, block(q)] = one_hot((site_ref[q : q + 1, :] & 63) == iota((NY, 128), 0))

    receive(in_box.at[0], 1)
    unpack(in_box.at[0], unpack_own, own)
    deposit = product(cell_mat)
    pack(lambda c: (base[block(c), :] - deposit(c)) * masks[block(c), :], pack_own, out_box.at[1])
    send(out_box.at[1], in_box.at[1], 2)

    def picks(o, target):
        for i in range(16):
            for q in range(CAP):
                there = lax.shift_right_logical(site_ref[q : q + 1, :], 6) == o * 16 + i
                there = one_hot(jnp.broadcast_to(there, (16, 128)))
                for r in range(NY // 16):
                    rows = slice(r * 16, r * 16 + 16)
                    target[i * NY + r * 16 : i * NY + r * 16 + 16, block(q)] = row_hot[rows, block(q)] * there

    def lay(o, source):
        rows = pl.ds(pl.multiple_of(o * 1024, 1024), 1024)
        two = dot(source[...], rhs[...])
        state[rows, :] = after[rows, :] - (two[:, 0:128] + two[:, 128:256])

    def two_blocks(o, carry):
        picks(2 * o + 1, pick_b)
        lay(2 * o, pick_a)
        picks(2 * o + 2, pick_a)
        lay(2 * o + 1, pick_b)
        return carry

    picks(0, pick_a)
    lax.fori_loop(0, 4, two_blocks, 0)
    halo_faces(1)
    halo_start(1)
    receive(in_box.at[1], 2)
    unpack(in_box.at[1], unpack_got, got)
    solve(True)
    pack(product(return_mat), pack_got, out_box.at[2])
    send(out_box.at[2], in_box.at[2], 3)

    halo_wait(1)
    stencil(1, 0, 128)
    gather(after, base)
    receive(in_box.at[2], 3)
    unpack(in_box.at[2], unpack_own, own)
    deposit = product(cell_mat)
    for c in range(CAP):
        columns_out[block(c), :] = base[block(c), :] - deposit(c)
    sent(out_one, 0)
    for k in range(3):
        sent(out_box.at[k], k + 1)


def settle(site, grid, rows, heat, out_hbm, heat_out, changed, sem):
    store_heat = pltpu.make_async_copy(heat, heat_out, sem.at[0])
    store_heat.start()

    def group(o, carry):
        for c in range(CAP):
            changed[pl.ds(site[c, o], 1), :] = rows[pl.ds(c * 128 + o, 1), :]
        return carry

    lax.fori_loop(0, GROUPS, group, 0, unroll=4)
    store = pltpu.make_async_copy(changed, out_hbm, sem.at[1])
    store.start()
    store_heat.wait()
    store.wait()


VMEM = pl.BlockSpec(memory_space=pltpu.VMEM)
SMEM = pl.BlockSpec(memory_space=pltpu.SMEM)
ANY = pl.BlockSpec(memory_space=pl.ANY)
HBM = pl.BlockSpec(memory_space=pltpu.HBM)


def local(u, flux, mix, site, first, stop, lookup, order, solver):
    def flat(table):
        return jnp.swapaxes(table.reshape(GROUPS, CAP), 0, 1)

    slots = flat(site)
    grid_shape = jax.ShapeDtypeStruct((CELLS, NZ), F32)
    slot_shape = jax.ShapeDtypeStruct((SLOTS, NZ), F32)
    slot_f32 = pltpu.VMEM((SLOTS, NZ), F32)
    slot_i32 = pltpu.VMEM((SLOTS, NZ), jnp.int32)
    square = pltpu.VMEM((SLOTS, SLOTS), BF16)
    grid, rows, heat = pl.pallas_call(
        transport,
        out_shape=(pltpu.VMEM((CELLS, NZ), F32), pltpu.VMEM((SLOTS, NZ), F32), pltpu.VMEM((SLOTS, NZ), F32)),
        in_specs=[HBM] * 8,
        out_specs=(VMEM, VMEM, VMEM),
        scratch_shapes=[
            pltpu.SMEM((CAP, GROUPS), jnp.int32),
            pltpu.VMEM((CAP, GROUPS), jnp.int32),
            pltpu.VMEM((CAP, GROUPS), jnp.int32),
            pltpu.VMEM((CAP, GROUPS), jnp.int32),
            pltpu.VMEM((1, SLOTS), jnp.int32),
            pltpu.VMEM((CELLS, NZ), F32),
            pltpu.VMEM((3, CELLS, NZ), BF16),
            pltpu.VMEM((2, CELLS, NZ), BF16),
            pltpu.VMEM((2, 2, NY, NZ), F32),
            pltpu.VMEM((2, 2, NX, NZ), F32),
            pltpu.VMEM((2, 2, NX, NZ), F32),
            slot_f32,
            slot_f32,
            slot_i32,
            slot_i32,
            slot_i32,
            slot_i32,
            square,
            square,
            square,
            pltpu.VMEM((SLOTS, 32), F32),
            pltpu.VMEM((2, SLOTS, 256), BF16),
            pltpu.VMEM((SLOTS, 256), BF16),
            pltpu.VMEM((NY, SLOTS), BF16),
            square,
            square,
            pltpu.VMEM((3, GROUPS, 4, NZ), F32),
            pltpu.VMEM((3, GROUPS, 4, NZ), F32),
            pltpu.VMEM((GROUPS, 5, NZ), F32),
            pltpu.VMEM((GROUPS, 5, NZ), F32),
            pltpu.SemaphoreType.DMA((9,)),
            pltpu.SemaphoreType.DMA((2, 4)),
            pltpu.SemaphoreType.DMA((2, 4)),
            pltpu.SemaphoreType.DMA((4,)),
            pltpu.SemaphoreType.DMA((4,)),
        ],
        compiler_params=pltpu.CompilerParams(
            collective_id=0, has_side_effects=True, vmem_limit_bytes=57 << 20
        ),
    )(
        u.reshape(CELLS, NZ),
        flux.reshape(3, CELLS, NZ),
        mix.reshape(2, CELLS, NZ),
        flat(first),
        flat(stop),
        slots,
        lookup.reshape(1, SLOTS),
        solver.reshape(SLOTS, 32),
    )
    grid, heat, _ = pl.pallas_call(
        settle,
        out_shape=(grid_shape, slot_shape, pltpu.VMEM((CELLS, NZ), F32)),
        in_specs=[SMEM, VMEM, VMEM, VMEM],
        out_specs=(ANY, ANY, VMEM),
        scratch_shapes=[pltpu.SemaphoreType.DMA((2,))],
        input_output_aliases={1: 2},
        compiler_params=pltpu.CompilerParams(vmem_limit_bytes=16 << 20),
    )(slots, grid, rows, heat)
    return grid.reshape(NX, NY, NZ), heat.reshape(1, 1, SLOTS, NZ)


def solution(mesh):
    placed = (
        P("gx", "gy", None),
        P(None, "gx", "gy", None),
        P(None, "gx", "gy", None),
        P("gx", "gy", None, None),
        P("gx", "gy", None, None),
        P("gx", "gy", None, None),
        P("gx", "gy", None),
        P("gx", "gy", None),
        P("gx", "gy", None, None, None),
    )
    return jax.shard_map(
        local,
        mesh=mesh,
        in_specs=placed,
        out_specs=(P("gx", "gy", None), P("gx", "gy", None, None)),
        check_vma=False,
    )
```

```python
import functools

import jax
import jax.numpy as jnp
from jax import lax
from jax.experimental import pallas as pl
from jax.experimental.pallas import tpu as pltpu
from jax.sharding import PartitionSpec as P

MESH = pl.DeviceIdType.MESH
F32 = jnp.float32
BF16 = jnp.bfloat16

NX, NY, NZ = 128, 64, 128
CELLS = NX * NY
GROUPS, CAP = 128, 8
SLOTS = GROUPS * CAP
HALF = 64

HOPS = (0, 1, 2, 1)
OFFSETS = sorted(
    [(a, b, c, d) for a in range(4) for b in range(4) for c in range(4) for d in range(2)][1:],
    key=lambda o: -(HOPS[o[0]] + HOPS[o[1]] + HOPS[o[2]] + 0.3 * o[3]),
)


def iota(shape, dim):
    return lax.broadcasted_iota(jnp.int32, shape, dim)


def dot(a, b):
    return jnp.dot(a, b, preferred_element_type=F32)


def parts_of(x):
    hi = x.astype(BF16)
    return hi, (x - hi.astype(F32)).astype(BF16)


def one_hot(mask):
    return jnp.where(mask, 1.0, 0.0).astype(BF16)


def tall(row):
    eye = iota((128, 128), 0) == iota((128, 128), 1)
    spread = jnp.where(eye, row.astype(F32), 0.0).astype(BF16)
    return dot(spread, jnp.ones((128, 128), BF16))


def rate_of(c, xm, xp, ym, yp, flux, mix):
    vx, vy, vz = flux
    kh, kv = mix
    lane = iota(c.shape, 1)
    zm = jnp.where(lane == 0, 0.0, pltpu.roll(c, 1, 1))
    zp = jnp.where(lane == NZ - 1, 0.0, pltpu.roll(c, NZ - 1, 1))
    xa, xb, ya, yb, za, zb = xp - c, c - xm, yp - c, c - ym, zp - c, c - zm
    advect = vx * jnp.where(vx > 0.0, xb, xa)
    advect += vy * jnp.where(vy > 0.0, yb, ya)
    advect += vz * jnp.where(vz > 0.0, zb, za)
    return c + 0.1 * (kh * ((xa - xb) + (ya - yb)) + kv * (za - zb) - advect)


def transport(
    u_hbm,
    flux_hbm,
    mix_hbm,
    first_hbm,
    stop_hbm,
    site_hbm,
    lookup_hbm,
    solver_hbm,
    after,
    columns_out,
    heat,
    site,
    first_ref,
    stop_ref,
    site_ref,
    lookup_row,
    state,
    flux,
    mix,
    xhalo,
    yhalo,
    yface,
    base,
    masks,
    pack_own,
    unpack_own,
    pack_got,
    unpack_got,
    lookup_mat,
    return_mat,
    cell_mat,
    solver,
    blocks,
    rhs,
    row_hot,
    pick_a,
    pick_b,
    out_box,
    in_box,
    out_one,
    in_one,
    load_sem,
    halo_send,
    halo_recv,
    send_sem,
    recv_sem,
):
    gx, gy = lax.axis_index("gx"), lax.axis_index("gy")
    me = gx * 8 + gy
    px, py = lax.div(gx, 4), lax.rem(gx, 4)
    pz, pc = lax.div(gy, 2), lax.rem(gy, 2)
    xs = [lax.rem(px + i, 4) for i in range(4)]
    ys = [lax.rem(py + i, 4) for i in range(4)]
    zs = [lax.rem(pz + i, 4) for i in range(4)]
    cs = [lax.rem(pc + i, 2) for i in range(2)]
    peers = [(xs[a] * 4 + ys[b], zs[c] * 2 + cs[d]) for a, b, c, d in OFFSETS]

    moves = (
        (first_hbm, first_ref),
        (stop_hbm, stop_ref),
        (site_hbm, site),
        (u_hbm, state),
        (site_hbm, site_ref),
        (lookup_hbm, lookup_row),
        (solver_hbm, solver),
        (flux_hbm, flux),
        (mix_hbm, mix),
    )
    loads = [
        pltpu.make_async_copy(source, target, load_sem.at[i])
        for i, (source, target) in enumerate(moves)
    ]
    for load in loads:
        load.start()
    barrier = pltpu.get_barrier_semaphore()
    for peer in peers:
        pl.semaphore_signal(barrier, inc=1, device_id=peer, device_id_type=MESH)

    lane = iota((128, 128), 1)

    def block(c):
        return slice(c * 128, c * 128 + 128)

    def indices(c, first, pack_ref, unpack_ref):
        shift = HALF if c >= 4 else 0
        pack_ref[block(c), :] = (lane + first + shift) & 127
        if unpack_ref is not None:
            unpack_ref[block(c), :] = (lane - first + shift) & 127

    def pack(value, index, box):
        for r in range(4):
            left, right = (
                jnp.take_along_axis(value(c), index[block(c), :], axis=1) for c in (r, r + 4)
            )
            box[:, r, :] = jnp.where(lane < HALF, left, right)

    def unpack(box, index, keep):
        for r in range(4):
            pair = box[:, r, :]
            for c in (r, r + 4):
                wide = jnp.take_along_axis(pair, index[block(c), :], axis=1)
                hi, lo = parts_of(jnp.where(keep(c), wide, 0.0))
                rhs[block(c), 0:128] = hi
                rhs[block(c), 128:256] = lo

    def own(c):
        return masks[block(c), :] > 0.0

    def got(c):
        return ((unpack_got[block(c), :] - (HALF if c >= 4 else 0)) & 127) < HALF

    def send(box, landing, k):
        for x, y in peers:
            pltpu.make_async_remote_copy(
                box.at[x * 8 + y],
                landing.at[me],
                send_sem.at[k],
                recv_sem.at[k],
                device_id=(x, y),
                device_id_type=MESH,
            ).start()
        landing[me] = box[me]

    def receive(landing, k):
        some = landing.at[pl.ds(0, GROUPS - 1)]
        pltpu.make_async_copy(some, some, recv_sem.at[k]).wait()

    def sent(box, k):
        some = box.at[pl.ds(0, GROUPS - 1)]
        pltpu.make_async_copy(some, some, send_sem.at[k]).wait()

    def halo_copies(step):
        low_x, high_x = state.at[pl.ds(0, NY)], state.at[pl.ds(CELLS - NY, NY)]
        low_y, high_y = yface.at[step, 0], yface.at[step, 1]
        plan = [
            (gx > 0, low_x, xhalo.at[step, 1], 1, (gx - 1, gy)),
            (gx < 15, high_x, xhalo.at[step, 0], 0, (gx + 1, gy)),
            (gy > 0, low_y, yhalo.at[step, 1], 3, (gx, gy - 1)),
            (gy < 7, high_y, yhalo.at[step, 0], 2, (gx, gy + 1)),
        ]
        return [
            (
                there,
                pltpu.make_async_remote_copy(
                    source,
                    target,
                    halo_send.at[step, side],
                    halo_recv.at[step, side],
                    device_id=device,
                    device_id_type=MESH,
                ),
            )
            for there, source, target, side, device in plan
        ]

    def halo_faces(step):
        def face(i, carry):
            yface[step, 0, pl.ds(i, 1), :] = state[pl.ds(i * NY, 1), :]
            yface[step, 1, pl.ds(i, 1), :] = state[pl.ds(i * NY + NY - 1, 1), :]
            return carry

        lax.fori_loop(0, NX, face, 0, unroll=8)

    def halo_start(step):
        for there, copy in halo_copies(step):

            @pl.when(there)
            def _():
                copy.start()

    def halo_wait(step):
        for there, copy in halo_copies(step):

            @pl.when(there)
            def _():
                copy.wait_send()

        for there, side in ((gx > 0, 0), (gx < 15, 1), (gy > 0, 2), (gy < 7, 3)):
            halo = xhalo.at[step, side] if side < 2 else yhalo.at[step, side - 2]

            @pl.when(there)
            def _():
                pltpu.make_async_copy(halo, halo, halo_recv.at[step, side]).wait()

    def stencil(step, start, stop):
        size = 16
        row = iota((size, NZ), 0)
        last = NY // size - 1

        def slab(i, below, above):
            for b in range(last + 1):
                o = pl.multiple_of(i * NY + b * size, size)
                here = pl.ds(o, size)
                c = state[here, :]
                if b > 0:
                    ym = state[pl.ds(o - 1, size), :]
                else:
                    ym = jnp.where(row == 0, yhalo[step, 0, pl.ds(i, 1), :], pltpu.roll(c, 1, 0))
                if b < last:
                    yp = state[pl.ds(o + 1, size), :]
                else:
                    edge = yhalo[step, 1, pl.ds(i, 1), :]
                    yp = jnp.where(row == size - 1, edge, pltpu.roll(c, size - 1, 0))
                after[here, :] = rate_of(
                    c,
                    below(b * size, size),
                    above(b * size, size),
                    ym,
                    yp,
                    [flux[d, here, :].astype(F32) for d in range(3)],
                    [mix[d, here, :].astype(F32) for d in range(2)],
                )

        def at(i):
            return lambda r, n: state[pl.ds(pl.multiple_of(i * NY + r, 16), n), :]

        def halo(side):
            return lambda r, n: xhalo[step, side, r : r + n, :]

        def inner(i, carry):
            slab(i, at(i - 1), at(i + 1))
            return carry

        if start == 0:
            slab(0, halo(0), at(1))
        lax.fori_loop(max(start, 1), min(stop, NX - 1), inner, 0, unroll=7)
        if stop == NX:
            slab(NX - 1, at(NX - 2), halo(1))

    def gather(source, target):
        def group(o, carry):
            for c in range(CAP):
                target[pl.ds(c * 128 + o, 1), :] = source[pl.ds(site[c, o], 1), :]
            return carry

        lax.fori_loop(0, GROUPS, group, 0, unroll=4)

    def solve(last):
        loops = dot(lookup_mat[...], rhs[...]).astype(BF16)
        for g in range(4):
            rows = slice(g * 256, g * 256 + 256)
            two = dot(blocks[0, rows, :], loops[rows])
            small = dot(blocks[1, rows, :], loops[rows, 0:128])
            rates = two[:, 0:128] + two[:, 128:256] + small
            if last:
                heat[rows, :] = rates
            hi, lo = parts_of(rates)
            rhs[rows, 0:128] = hi
            rhs[rows, 128:256] = lo

    def product(matrix):
        two = dot(matrix[...], rhs[...])
        return lambda c: two[block(c), 0:128] + two[block(c), 128:256]

    loads[0].wait()
    loads[1].wait()
    table = jnp.zeros((128, 128), F32)
    for c in range(CAP):
        first, stop = tall(first_ref[c : c + 1, :]), tall(stop_ref[c : c + 1, :])
        table = jnp.where(lane == c, first, table)
        first, stop = first.astype(jnp.int32), stop.astype(jnp.int32)
        masks[block(c), :] = jnp.where((lane >= first) & (lane < stop), 1.0, 0.0)
        indices(c, first, pack_own, None)
    out_one[:, 4, :] = table
    loads[2].wait()
    loads[3].wait()
    gather(state, base)
    pack(lambda c: base[block(c), :] * masks[block(c), :], pack_own, out_one)

    pl.semaphore_wait(barrier, GROUPS - 1)
    send(out_one, in_one, 0)
    halo_faces(0)
    halo_start(0)
    for edge, halo, side in ((gx == 0, xhalo, 0), (gx == 15, xhalo, 1), (gy == 0, yhalo, 0), (gy == 7, yhalo, 1)):

        @pl.when(edge)
        def _():
            halo[:, side] = jnp.zeros_like(halo[:, side])

    for c in range(CAP):
        unpack_own[block(c), :] = (2 * lane - pack_own[block(c), :]) & 127

    loads[5].wait()
    lookup = lookup_row[...]
    lookup = jnp.where(lookup < SLOTS, (lookup & 7) * 128 + lax.shift_right_logical(lookup, 3), SLOTS)

    def build(o, carry):
        rows = pl.ds(pl.multiple_of(o * 128, 128), 128)
        return_mat[rows, :] = one_hot(lookup == iota((128, SLOTS), 0) + o * 128)
        return carry

    lax.fori_loop(0, 8, build, 0)
    for o in range(8):
        piece = lookup[:, block(o)]
        column = (tall(lax.shift_right_logical(piece, 3)) * 8.0 + tall(piece & 7)).astype(jnp.int32)
        for c in range(CAP):
            lookup_mat[block(o), block(c)] = one_hot(column == lane + c * 128)
    loads[6].wait()
    tile = one_hot(iota((32, 256), 1) % 32 == iota((32, 256), 0))
    own_block = (iota((SLOTS, 256), 0) // 32) % 8 == iota((SLOTS, 256), 1) // 32
    for part, piece in enumerate(parts_of(solver[...])):
        blocks[part] = jnp.where(own_block, dot(piece, tile), 0.0).astype(BF16)

    for load in (loads[4], loads[7], loads[8]):
        load.wait()
    halo_wait(0)
    stencil(0, 0, 29)
    receive(in_one, 0)
    sources = in_one[:, 4, :]
    for c in range(CAP):
        first = dot(jnp.where(lane == c, sources, 0.0).astype(BF16), jnp.ones((128, 128), BF16))
        indices(c, first.astype(jnp.int32), pack_got, unpack_got)
    unpack(in_one, unpack_got, got)
    solve(False)
    pack(product(return_mat), pack_got, out_box.at[0])
    send(out_box.at[0], in_box.at[0], 1)

    stencil(0, 29, 128)
    gather(after, base)
    for o in range(CAP):
        piece = site_ref[o : o + 1, :]
        column = (tall(lax.shift_right_logical(piece, 6)) * 64.0 + tall(piece & 63)).astype(jnp.int32)
        for q in range(CAP):
            cell_mat[block(o), block(q)] = one_hot(column == site_ref[q : q + 1, :])
    for q in range(CAP):
        row_hot[:, block(q)] = one_hot((site_ref[q : q + 1, :] & 63) == iota((NY, 128), 0))

    receive(in_box.at[0], 1)
    unpack(in_box.at[0], unpack_own, own)
    deposit = product(cell_mat)
    pack(lambda c: (base[block(c), :] - deposit(c)) * masks[block(c), :], pack_own, out_box.at[1])
    send(out_box.at[1], in_box.at[1], 2)

    def picks(o, target):
        for i in range(16):
            for q in range(CAP):
                there = lax.shift_right_logical(site_ref[q : q + 1, :], 6) == o * 16 + i
                there = one_hot(jnp.broadcast_to(there, (16, 128)))
                for r in range(NY // 16):
                    rows = slice(r * 16, r * 16 + 16)
                    target[i * NY + r * 16 : i * NY + r * 16 + 16, block(q)] = row_hot[rows, block(q)] * there

    def lay(o, source):
        rows = pl.ds(pl.multiple_of(o * 1024, 1024), 1024)
        two = dot(source[...], rhs[...])
        state[rows, :] = after[rows, :] - (two[:, 0:128] + two[:, 128:256])

    def two_blocks(o, carry):
        picks(2 * o + 1, pick_b)
        lay(2 * o, pick_a)
        picks(2 * o + 2, pick_a)
        lay(2 * o + 1, pick_b)
        return carry

    picks(0, pick_a)
    lax.fori_loop(0, 4, two_blocks, 0)
    halo_faces(1)
    halo_start(1)
    receive(in_box.at[1], 2)
    unpack(in_box.at[1], unpack_got, got)
    solve(True)
    pack(product(return_mat), pack_got, out_box.at[2])
    send(out_box.at[2], in_box.at[2], 3)

    halo_wait(1)
    stencil(1, 0, 128)
    gather(after, base)
    receive(in_box.at[2], 3)
    unpack(in_box.at[2], unpack_own, own)
    deposit = product(cell_mat)
    for c in range(CAP):
        columns_out[block(c), :] = base[block(c), :] - deposit(c)
    sent(out_one, 0)
    for k in range(3):
        sent(out_box.at[k], k + 1)


def settle(site, grid, rows, heat, out_hbm, heat_out, changed, sem):
    store_heat = pltpu.make_async_copy(heat, heat_out, sem.at[0])
    store_heat.start()

    def group(o, carry):
        for c in range(CAP):
            changed[pl.ds(site[c, o], 1), :] = rows[pl.ds(c * 128 + o, 1), :]
        return carry

    lax.fori_loop(0, GROUPS, group, 0, unroll=4)
    store = pltpu.make_async_copy(changed, out_hbm, sem.at[1])
    store.start()
    store_heat.wait()
    store.wait()


VMEM = pl.BlockSpec(memory_space=pltpu.VMEM)
SMEM = pl.BlockSpec(memory_space=pltpu.SMEM)
ANY = pl.BlockSpec(memory_space=pl.ANY)
HBM = pl.BlockSpec(memory_space=pltpu.HBM)


def local(u, flux, mix, site, first, stop, lookup, order, solver):
    def flat(table):
        return jnp.swapaxes(table.reshape(GROUPS, CAP), 0, 1)

    slots = flat(site)
    grid_shape = jax.ShapeDtypeStruct((CELLS, NZ), F32)
    slot_shape = jax.ShapeDtypeStruct((SLOTS, NZ), F32)
    slot_f32 = pltpu.VMEM((SLOTS, NZ), F32)
    slot_i32 = pltpu.VMEM((SLOTS, NZ), jnp.int32)
    square = pltpu.VMEM((SLOTS, SLOTS), BF16)
    grid, rows, heat = pl.pallas_call(
        transport,
        out_shape=(pltpu.VMEM((CELLS, NZ), F32), pltpu.VMEM((SLOTS, NZ), F32), pltpu.VMEM((SLOTS, NZ), F32)),
        in_specs=[HBM] * 8,
        out_specs=(VMEM, VMEM, VMEM),
        scratch_shapes=[
            pltpu.SMEM((CAP, GROUPS), jnp.int32),
            pltpu.VMEM((CAP, GROUPS), jnp.int32),
            pltpu.VMEM((CAP, GROUPS), jnp.int32),
            pltpu.VMEM((CAP, GROUPS), jnp.int32),
            pltpu.VMEM((1, SLOTS), jnp.int32),
            pltpu.VMEM((CELLS, NZ), F32),
            pltpu.VMEM((3, CELLS, NZ), BF16),
            pltpu.VMEM((2, CELLS, NZ), BF16),
            pltpu.VMEM((2, 2, NY, NZ), F32),
            pltpu.VMEM((2, 2, NX, NZ), F32),
            pltpu.VMEM((2, 2, NX, NZ), F32),
            slot_f32,
            slot_f32,
            slot_i32,
            slot_i32,
            slot_i32,
            slot_i32,
            square,
            square,
            square,
            pltpu.VMEM((SLOTS, 32), F32),
            pltpu.VMEM((2, SLOTS, 256), BF16),
            pltpu.VMEM((SLOTS, 256), BF16),
            pltpu.VMEM((NY, SLOTS), BF16),
            square,
            square,
            pltpu.VMEM((3, GROUPS, 4, NZ), F32),
            pltpu.VMEM((3, GROUPS, 4, NZ), F32),
            pltpu.VMEM((GROUPS, 5, NZ), F32),
            pltpu.VMEM((GROUPS, 5, NZ), F32),
            pltpu.SemaphoreType.DMA((9,)),
            pltpu.SemaphoreType.DMA((2, 4)),
            pltpu.SemaphoreType.DMA((2, 4)),
            pltpu.SemaphoreType.DMA((4,)),
            pltpu.SemaphoreType.DMA((4,)),
        ],
        compiler_params=pltpu.CompilerParams(
            collective_id=0, has_side_effects=True, vmem_limit_bytes=57 << 20
        ),
    )(
        u.reshape(CELLS, NZ),
        flux.reshape(3, CELLS, NZ),
        mix.reshape(2, CELLS, NZ),
        flat(first),
        flat(stop),
        slots,
        lookup.reshape(1, SLOTS),
        solver.reshape(SLOTS, 32),
    )
    grid, heat, _ = pl.pallas_call(
        settle,
        out_shape=(grid_shape, slot_shape, pltpu.VMEM((CELLS, NZ), F32)),
        in_specs=[SMEM, VMEM, VMEM, VMEM],
        out_specs=(ANY, ANY, VMEM),
        scratch_shapes=[pltpu.SemaphoreType.DMA((2,))],
        input_output_aliases={1: 2},
        compiler_params=pltpu.CompilerParams(vmem_limit_bytes=16 << 20),
    )(slots, grid, rows, heat)
    return grid.reshape(NX, NY, NZ), heat.reshape(1, 1, SLOTS, NZ)


def solution(mesh):
    placed = (
        P("gx", "gy", None),
        P(None, "gx", "gy", None),
        P(None, "gx", "gy", None),
        P("gx", "gy", None, None),
        P("gx", "gy", None, None),
        P("gx", "gy", None, None),
        P("gx", "gy", None),
        P("gx", "gy", None),
        P("gx", "gy", None, None, None),
    )
    return jax.shard_map(
        local,
        mesh=mesh,
        in_specs=placed,
        out_specs=(P("gx", "gy", None), P("gx", "gy", None, None)),
        check_vma=False,
    )
```
